32 devices in a mesh: group: 4 (over z), dp: 8 (over y, x, core).
Axes of the slice: x: 2, y: 2, z: 4, core: 2. Of those that a mesh axis runs over, the one named last changes fastest.
Arguments:
- queries: bfloat16 [64, 128, 512], P(('group', 'dp')), may hold values from -256 to 256
- passages: bfloat16 [192, 128, 512], P(('group', 'dp')), may hold values from -6 to 6
- candidates: int32 [64, 16], replicated, may hold values from 0 to 191, as said below
- positives: int32 [64, 128], P(('group', 'dp')), may hold values from 0 to 2047
- row_weight: float32 [64, 128], P(('group', 'dp')), may hold values from 0.25 to 4
- owner_map: int32 [192], replicated, may hold values from 0 to 191, as said below
Outputs:
- grad_query: bfloat16 [64, 128, 512], P(('group', 'dp'))
- grad_passage: bfloat16 [192, 128, 512], P(('group', 'dp'))
The draws below stay inside these ranges and needn't reach their ends.
Inputs may be any that keep to these rules, and one draw needn't show every extreme that they name: `owner_map`: A permutation: entry i is the row block of passages that holds block id i. `candidates`: each row lists 16 different block ids: 12 held by devices of the query block's own group, the others held by devices of other groups with the same dp index. Over all query blocks of one device, at most 2 distinct listed blocks lie on any one device of its group and at most 2 on the devices of any one other group; for every device both bounds are reached.
All inputs are finite; a program needn't handle non-finite values.
Results may differ from the reference program's by a relative error of at most 0.0057.
Values may be sent and summed in bfloat16 or wider, within the bound.
No kernel may reach another device: no remote copies, remote signals or barrier semaphores. Data moves between devices by JAX's collectives and lax.ppermute only.
A program may use at most 128 MiB of HBM per device.

```python
import math
import jax
import jax.numpy as jnp
from jax import lax

D = 512
BR = 128
NCAND = 16
NLOCAL = 12
QB_DEV = 2
PB_DEV = 6
NREMOTE = 4
CAPL = 2
CAPR = 2
QBLOCKS = 64
NBLK = 192
N_GROUP = 4
N_DP = 8
DEVICES = 32


def routing_tables(key):
    owner_map = jax.random.permutation(jax.random.fold_in(key, 7), NBLK).astype(jnp.int32)
    block_at = jnp.argsort(owner_map).astype(jnp.int32)
    hot_peer = jax.random.randint(jax.random.fold_in(key, 8), (N_GROUP,), 0, N_DP)
    local_peer = jnp.repeat(jnp.arange(N_DP, dtype=jnp.int32), CAPL)
    remote_group = jnp.repeat(jnp.arange(N_GROUP, dtype=jnp.int32), CAPR)

    def one_device(device):
        device_key = jax.random.fold_in(jax.random.fold_in(key, 9), device)
        group_index = device // N_DP
        column = device % N_DP
        local_rank = jax.random.randint(jax.random.fold_in(device_key, 1), (N_DP, PB_DEV), 0, 65536) * PB_DEV + jnp.arange(PB_DEV, dtype=jnp.int32)[None, :]
        local_slot = jnp.argsort(local_rank, axis=1)[:, :CAPL].astype(jnp.int32)
        remote_rank = jax.random.randint(jax.random.fold_in(device_key, 2), (N_GROUP, PB_DEV), 0, 65536) * PB_DEV + jnp.arange(PB_DEV, dtype=jnp.int32)[None, :]
        remote_slot = jnp.argsort(remote_rank, axis=1)[:, :CAPR].astype(jnp.int32)
        local_pos = ((group_index * N_DP + jnp.arange(N_DP, dtype=jnp.int32))[:, None] * PB_DEV + local_slot).reshape(-1)
        remote_pos = ((jnp.arange(N_GROUP, dtype=jnp.int32) * N_DP + column)[:, None] * PB_DEV + remote_slot).reshape(-1)
        hot_remote = (group_index + 1 + jax.random.randint(jax.random.fold_in(device_key, 3), (), 0, N_GROUP - 1)) % N_GROUP

        def one_block(block):
            block_key = jax.random.fold_in(device_key, 100 + block)
            local_score = jax.random.randint(jax.random.fold_in(block_key, 1), (N_DP * CAPL,), 0, 65536) * 1024 + jnp.arange(N_DP * CAPL, dtype=jnp.int32)
            local_score = local_score + jnp.where(local_peer == hot_peer[group_index], 134217728, 0)
            pick_local = jnp.argsort(-local_score)[:NLOCAL]
            remote_score = jax.random.randint(jax.random.fold_in(block_key, 2), (N_GROUP * CAPR,), 0, 65536) * 1024 + jnp.arange(N_GROUP * CAPR, dtype=jnp.int32)
            remote_score = remote_score + jnp.where(remote_group == hot_remote, 134217728, 0)
            remote_score = jnp.where(remote_group == group_index, -1, remote_score)
            pick_remote = jnp.argsort(-remote_score)[:NREMOTE]
            chosen = jnp.concatenate([local_pos[pick_local], remote_pos[pick_remote]])
            shuffle = jax.random.permutation(jax.random.fold_in(block_key, 3), NCAND)
            return block_at[chosen[shuffle]]
        return jax.vmap(one_block)(jnp.arange(QB_DEV, dtype=jnp.int32))
    lists = jax.vmap(one_device)(jnp.arange(DEVICES, dtype=jnp.int32))
    return (owner_map, lists.reshape(QBLOCKS, NCAND).astype(jnp.int32))


def draw_owner_map(key, part):
    return routing_tables(key)[0]


def draw_candidates(key, part):
    return routing_tables(key)[1]


def draw_queries(key, part):
    values = jax.random.truncated_normal(jax.random.fold_in(key, 1), -6.0, 6.0, (QBLOCKS, BR, D), jnp.float32)
    return values.astype(jnp.bfloat16)


def with_ends(entries, own_key, low, top_value):
    spot = [jax.random.randint(jax.random.fold_in(own_key, axis), (), 0, length) for axis, length in enumerate(entries.shape)]
    main_axis = entries.shape.index(max(entries.shape))
    beside = spot[:main_axis] + [(spot[main_axis] + 1) % entries.shape[main_axis]] + spot[main_axis + 1:]
    return entries.at[tuple(spot)].set(low).at[tuple(beside)].set(top_value)


def block_scale(own_key, extent, cuts, low, largest):
    gain, own = 1.0, jax.random.fold_in(own_key, 6)
    for position, blocks in cuts:
        draws = jnp.exp(jax.random.uniform(jax.random.fold_in(own, position), (blocks,), jnp.float32, low / len(cuts), largest / len(cuts)))
        gain = gain * jnp.repeat(draws, extent[position] // blocks).reshape([-1 if axis == position else 1 for axis in range(len(extent))])
    return gain


def normal_values(own_key, dims, scale, bound, shards=(), kind=jnp.bfloat16):
    values = jax.random.normal(own_key, dims, jnp.float32) * scale
    if len(shards) > 0:
        values = block_scale(own_key, dims, shards, -0.22, 0.18) * values
    return jnp.clip(values, min=-bound, max=bound).astype(kind)


def setup_inputs(seed: int = 0) -> dict:
    key_of = jax.random.split(jax.random.key(seed), 7)
    return {
        "queries": draw_queries(jax.random.fold_in(key_of[6], 71), 0),
        "passages": normal_values(key_of[1], (NBLK, BR, D), 1.0, 6.0, ((0, 32),)),
        "candidates": draw_candidates(jax.random.fold_in(key_of[6], 71), 0),
        "positives": with_ends(jax.random.randint(key_of[3], (QBLOCKS, BR), 0, NCAND * BR), jax.random.fold_in(key_of[3], 1), 0, (NCAND * BR) - 1).astype(jnp.int32),
        "row_weight": jnp.clip(jnp.exp(math.log(4.0) - 2.7725887 * jax.random.uniform(key_of[4], (QBLOCKS, BR), jnp.float32) ** block_scale(key_of[4], (QBLOCKS, BR), ((0, 32),), -0.2, 0.2)), 0.25, 4.0),
        "owner_map": draw_owner_map(jax.random.fold_in(key_of[6], 71), 0),
    }


def reference(queries, passages, candidates, positives, row_weight, owner_map):
    score_scale = 3.0 / math.sqrt(D)
    listing = jnp.arange(QB_DEV * NCAND, dtype=jnp.int32)
    target_index = jnp.arange(NCAND * BR, dtype=jnp.int32)

    def device_step(grad_sum, device):
        start = (device * QB_DEV).astype(jnp.int32)
        query_part = lax.dynamic_slice_in_dim(queries, start, QB_DEV, 0).astype(jnp.float32)
        listed = lax.dynamic_slice_in_dim(candidates, start, QB_DEV, 0)
        target_rows = lax.dynamic_slice_in_dim(positives, start, QB_DEV, 0)
        weight_rows = lax.dynamic_slice_in_dim(row_weight, start, QB_DEV, 0)
        positions = jnp.take(owner_map, listed.reshape(-1)).astype(jnp.int32)
        candidate = jnp.take(passages, positions, axis=0).astype(jnp.float32).reshape(QB_DEV, NCAND, BR, D)
        scores = jnp.einsum('brd,bkjd->brkj', query_part, candidate) * score_scale
        probability = jax.nn.softmax(scores.reshape(QB_DEV, BR, NCAND * BR), axis=-1)
        target = (target_index[None, None, :] == target_rows[:, :, None]).astype(jnp.float32)
        dscore = ((probability - target) * (weight_rows[:, :, None] * score_scale)).astype(jnp.bfloat16)
        dscore = lax.optimization_barrier(dscore).astype(jnp.float32).reshape(QB_DEV, BR, NCAND, BR)
        grad_query = jnp.einsum('brkj,bkjd->brd', dscore, candidate).astype(jnp.bfloat16)
        pair_terms = jnp.einsum('brkj,brd->bkjd', dscore, query_part).reshape(QB_DEV * NCAND, BR, D)
        same_block = positions[:, None] == positions[None, :]
        merged = jnp.einsum('lm,mxd->lxd', same_block.astype(jnp.float32), pair_terms, precision=lax.Precision.HIGHEST)
        rounded = lax.optimization_barrier(merged.astype(jnp.bfloat16)).astype(jnp.float32)
        earlier = same_block & (listing[None, :] < listing[:, None])
        unique = jnp.logical_not(jnp.any(earlier, axis=1)).astype(jnp.float32)
        grad_sum = grad_sum.at[positions].add(rounded * unique[:, None, None])
        return (grad_sum, grad_query)
    grad_sum, grad_query = lax.scan(device_step, jnp.zeros((NBLK, BR, D), jnp.float32), jnp.arange(DEVICES, dtype=jnp.int32))
    return (grad_query.reshape(QBLOCKS, BR, D), grad_sum.astype(jnp.bfloat16))
```

```python
import functools
import math

import jax
import jax.numpy as jnp
from jax import lax
from jax.experimental import pallas as pl
from jax.experimental.pallas import tpu as pltpu
from jax.sharding import PartitionSpec as P

NLOCAL = 12
VMEM_BYTES = 32 * 1024 * 1024


def swap(x, axis, mask):
    size = lax.axis_size(axis)
    return lax.ppermute(x, axis, [(i, i ^ mask) for i in range(size)])


def slot_table(listing, cap):
    listed = jnp.max(listing, axis=1) >= 0
    blocks = listed.shape[1]
    number = jnp.arange(blocks, dtype=jnp.int32)
    ahead = listed[:, None, :] & (number[None, None, :] < number[None, :, None])
    rank = jnp.sum(ahead.astype(jnp.int32), axis=2)
    taken = listed[:, None, :] & (
        rank[:, None, :] == jnp.arange(cap, dtype=jnp.int32)[None, :, None]
    )
    block = jnp.max(jnp.where(taken, number, 0), axis=2)
    entry = jnp.max(jnp.where(taken[:, None], listing[:, :, None, :], -1), axis=3)
    return block, entry.reshape(entry.shape[0], -1)


def serve_kernel(sources, me, block, passages, *rest):
    outs, sems = rest[:-1], rest[-1]
    copies = []
    for out, pieces in zip(outs, sources(me)):
        for piece, (owner, slot) in enumerate(pieces):
            copies.append(
                pltpu.make_async_copy(
                    passages.at[block[owner, slot]], out.at[piece], sems.at[len(copies)]
                )
            )
    for copy in copies:
        copy.start()
    for copy in copies:
        copy.wait()


def serve(sources, counts, me, block, passages):
    smem = pl.BlockSpec(memory_space=pltpu.SMEM)
    hbm = pl.BlockSpec(memory_space=pl.ANY)
    return pl.pallas_call(
        functools.partial(serve_kernel, sources),
        out_shape=[
            jax.ShapeDtypeStruct((count,) + passages.shape[1:], passages.dtype) for count in counts
        ],
        in_specs=[smem, smem, hbm],
        out_specs=[hbm] * len(counts),
        scratch_shapes=[pltpu.SemaphoreType.DMA((sum(counts),))],
        compiler_params=pltpu.CompilerParams(vmem_limit_bytes=VMEM_BYTES),
    )(me, block, passages)


def masked_scores(scale, entry, holder, cap, query, block_rows, pieces):
    slots = pieces.shape[0] // block_rows
    scores = (
        lax.dot_general(
            query, pieces, (((1,), (1,)), ((), ())), preferred_element_type=jnp.float32
        )
        * scale
    )
    for block in range(query.shape[0] // block_rows):
        for slot in range(slots):
            listing = entry[holder, block * cap + slot]
            bias = jnp.where(listing >= 0, 0.0, -jnp.inf).astype(jnp.float32)
            rows = slice(block * block_rows, (block + 1) * block_rows)
            columns = slice(slot * block_rows, (slot + 1) * block_rows)
            yield block, slot, listing, scores[rows, columns] + bias


def holders_of(me, columns, groups):
    group, column = me[0], me[1]
    near = [group * columns + peer for peer in range(columns)]
    far = [(group ^ mask) * columns + column for mask in range(1, groups)]
    return near, far


def held_pieces(me, columns, groups, near_ref, far_refs):
    near, far = holders_of(me, columns, groups)
    width = near_ref.shape[-1]
    caps = near_ref.shape[0] // columns
    for peer, holder in enumerate(near):
        yield holder, near_ref[peer * caps : (peer + 1) * caps].reshape(-1, width)
    for ref, holder in zip(far_refs, far):
        yield holder, ref[...].reshape(-1, width)


def stats_kernel(
    scale, cap, columns, groups, me, entry, queries, weight, positives, near, *rest
):
    far, stat, scores_ref, peak_ref = rest[: groups - 1], rest[-3], rest[-2], rest[-1]
    query_blocks, block_rows, width = queries.shape
    rows = query_blocks * block_rows
    query = queries[...].reshape(rows, width)
    peak_ref[...] = jnp.full_like(peak_ref, -jnp.inf)
    at = 0
    for holder, pieces in held_pieces(me, columns, groups, near, far):
        for block, slot, _, part in masked_scores(
            scale, entry, holder, cap, query, block_rows, pieces
        ):
            mine = slice(block * block_rows, (block + 1) * block_rows)
            scores_ref[at + slot, mine] = part
            peak_ref[mine] = jnp.maximum(peak_ref[mine], part)
        at += pieces.shape[0] // block_rows
    peak = jnp.max(peak_ref[...], axis=1, keepdims=True)
    total = jnp.zeros((rows, block_rows), jnp.float32)
    for index in range(at):
        total = total + jnp.exp(scores_ref[index] - peak)
    total = jnp.sum(total, axis=1, keepdims=True)
    lane = lax.broadcasted_iota(jnp.int32, (rows, 128), 1)
    turned = jnp.where(lane == 0, peak, total).T
    stat[...] = jnp.zeros_like(stat)
    stat[0:2] = turned[0:2]
    for block in range(query_blocks):
        mine = slice(block * block_rows, (block + 1) * block_rows)
        stat[2:3, mine] = weight[block : block + 1] * scale
        stat[3:4, mine] = positives[block : block + 1].astype(jnp.float32)


def query_kernel(scale, cap, columns, groups, me, entry, queries, stat, near, *rest):
    far, out, total, dscore_ref = rest[: groups - 1], rest[-3], rest[-2], rest[-1]
    query_blocks, block_rows, width = queries.shape
    rows = query_blocks * block_rows
    query = queries[...].reshape(rows, width)
    turned = jnp.concatenate(
        [stat[...], jnp.zeros((128 - stat.shape[0], rows), jnp.float32)], axis=0
    ).T
    peak, inverse = turned[:, 0:1], 1.0 / turned[:, 1:2]
    weight, positive = turned[:, 2:3], turned[:, 3:4]
    place = lax.broadcasted_iota(jnp.int32, (block_rows, block_rows), 1)
    total[...] = jnp.zeros_like(total)
    for holder, pieces in held_pieces(me, columns, groups, near, far):
        for block, slot, listing, part in masked_scores(
            scale, entry, holder, cap, query, block_rows, pieces
        ):
            mine = slice(block * block_rows, (block + 1) * block_rows)
            number = (place + listing * block_rows).astype(jnp.float32)
            target = jnp.where(positive[mine] == number, 1.0, 0.0)
            chance = jnp.exp(part - peak[mine]) * inverse[mine]
            dscore_ref[mine, slot * block_rows : (slot + 1) * block_rows] = (
                (chance - target) * weight[mine]
            ).astype(jnp.bfloat16)
        total[...] += jnp.dot(
            dscore_ref[:, : pieces.shape[0]], pieces, preferred_element_type=jnp.float32
        )
    out[...] = total[...].reshape(out.shape).astype(out.dtype)


def passage_kernel(
    scale, cap, near_cap, far_cap, columns, groups, me, block, entry, passages, even, odd, *rest
):
    far_count = groups - 1
    far, near_stats = rest[:far_count], rest[far_count : far_count + columns // 2]
    far_stats = rest[far_count + columns // 2 : 2 * far_count + columns // 2]
    out, total = rest[-2], rest[-1]
    query_blocks, block_rows, width = even.shape[1:]
    rows = query_blocks * block_rows
    group, column = me[0], me[1]
    units = []
    for pair in range(columns // 2):
        for core, side in enumerate((even, odd)):
            owner = group * columns + (column ^ (2 * pair + core))
            units.append((owner, near_cap, side.at[pair], near_stats[pair].at[core]))
    for mask in range(1, groups):
        owner = (group ^ mask) * columns + column
        units.append((owner, far_cap, far[mask - 1], far_stats[mask - 1]))
    total[...] = jnp.zeros_like(total)
    lane = lax.broadcasted_iota(jnp.int32, (1, rows), 1)
    place = lax.broadcasted_iota(jnp.int32, (block_rows, rows), 0)
    for owner, slots, query_ref, stat in units:
        query = query_ref[...].reshape(rows, width)
        peak, inverse = stat[0:1], 1.0 / stat[1:2]
        weight, positive = stat[2:3], stat[3:4]
        held = [block[owner, slot] for slot in range(slots)]
        mine = jnp.concatenate([passages[index] for index in held], axis=0)
        scores = (
            lax.dot_general(
                mine, query, (((1,), (1,)), ((), ())), preferred_element_type=jnp.float32
            )
            * scale
        )
        parts = []
        for slot in range(slots):
            listing = jnp.full((1, rows), entry[owner, slot], jnp.int32)
            for query_block in range(1, query_blocks):
                listing = jnp.where(
                    lane >= query_block * block_rows, entry[owner, query_block * cap + slot], listing
                )
            bias = jnp.where(listing >= 0, 0.0, -jnp.inf)
            number = (place + listing * block_rows).astype(jnp.float32)
            part = scores[slot * block_rows : (slot + 1) * block_rows] + bias
            target = jnp.where(positive == number, 1.0, 0.0)
            chance = jnp.exp(part - peak) * inverse
            parts.append(((chance - target) * weight).astype(jnp.bfloat16))
        term = jnp.dot(
            jnp.concatenate(parts, axis=0), query, preferred_element_type=jnp.float32
        ).astype(jnp.bfloat16)
        for slot, index in enumerate(held):
            total[index] += term[slot * block_rows : (slot + 1) * block_rows].astype(jnp.float32)
    out[...] = total[...].astype(out.dtype)


def call(kernel, out, scratch, flops, smem_args, vmem_args):
    return pl.pallas_call(
        kernel,
        out_shape=out,
        in_specs=[pl.BlockSpec(memory_space=pltpu.SMEM)] * len(smem_args)
        + [pl.BlockSpec(memory_space=pltpu.VMEM)] * len(vmem_args),
        out_specs=pl.BlockSpec(memory_space=pltpu.VMEM),
        scratch_shapes=scratch,
        compiler_params=pltpu.CompilerParams(vmem_limit_bytes=VMEM_BYTES),
        cost_estimate=pl.CostEstimate(
            flops=flops,
            bytes_accessed=sum(math.prod(a.shape) * a.dtype.itemsize for a in vmem_args),
            transcendentals=0,
        ),
    )(*smem_args, *vmem_args)


def gather_columns(x, axis):
    size = lax.axis_size(axis)
    half = x.shape[0] // 2
    held = {0: x}
    for mask in range(2, size, 2):
        high = 1 << (mask.bit_length() - 1)
        low = mask & -mask
        if high == low:
            held[mask] = swap(x, axis, mask)
        else:
            held[mask] = jnp.concatenate(
                [
                    swap(held[mask ^ high][:half], axis, high),
                    swap(held[mask ^ low][half:], axis, low),
                ]
            )
    even = jnp.stack([held[mask] for mask in range(0, size, 2)])
    return even, swap(even, axis, 1)


def gather_groups(x, axis):
    held = {0: x}
    mask = lax.axis_size(axis) - 1
    while mask:
        held.update({at ^ mask: swap(piece, axis, mask) for at, piece in list(held.items())})
        mask >>= 1
    return [held[at] for at in range(1, lax.axis_size(axis))]


def shards(queries, passages, candidates, positives, row_weight, owner_map):
    columns = lax.axis_size("dp")
    groups = lax.axis_size("group")
    my_group = lax.axis_index("group").astype(jnp.int32)
    my_column = lax.axis_index("dp").astype(jnp.int32)
    device = my_group * columns + my_column
    me = jnp.stack([my_group, my_column])
    query_blocks, block_rows, width = queries.shape
    rows = query_blocks * block_rows
    blocks = passages.shape[0]
    listed = candidates.shape[1]
    near_cap = (NLOCAL + columns - 1) // columns
    far_cap = (listed - NLOCAL + groups - 2) // (groups - 1)
    cap = max(near_cap, far_cap)
    devices = columns * groups
    scale = 3.0 / math.sqrt(width)

    far_queries = gather_groups(queries, "group")
    even, odd = gather_columns(queries, "dp")

    number = jnp.arange(listed, dtype=jnp.int32)
    held_at = device * blocks + jnp.arange(blocks, dtype=jnp.int32)
    block_id = jnp.sum(
        jnp.where(
            owner_map[None, :] == held_at[:, None],
            jnp.arange(owner_map.shape[0], dtype=jnp.int32)[None, :],
            0,
        ),
        axis=1,
    )
    asked = jnp.max(
        jnp.where(
            candidates[:, None, :] == block_id[None, :, None], number[None, None, :], -1
        ),
        axis=2,
    ).reshape(devices, query_blocks, blocks)
    asked_block, asked_entry = slot_table(asked, cap)

    def far_sources(me):
        _, far = holders_of(me, columns, groups)
        return [[(owner, slot) for slot in range(far_cap)] for owner in far]

    def near_sources(me):
        near, _ = holders_of(me, columns, groups)
        return [[(owner, slot) for owner in near for slot in range(near_cap)]]

    far_out = serve(far_sources, [far_cap] * (groups - 1), me, asked_block, passages)
    far_blocks = [swap(piece, "group", mask + 1) for mask, piece in enumerate(far_out)]
    (near_out,) = serve(near_sources, [columns * near_cap], me, asked_block, passages)
    near_blocks = lax.all_to_all(near_out, "dp", split_axis=0, concat_axis=0, tiled=True)

    my_lists = lax.dynamic_slice_in_dim(candidates, device * query_blocks, query_blocks, 0)
    my_places = jnp.take(owner_map, my_lists)
    place = jnp.arange(devices * blocks, dtype=jnp.int32).reshape(devices, blocks)
    wanted = jnp.max(
        jnp.where(
            my_places[None, :, None, :] == place[:, None, :, None], number, -1
        ),
        axis=3,
    )
    _, my_entry = slot_table(wanted, cap)

    slots = columns * near_cap + (groups - 1) * far_cap
    flops = 2 * rows * slots * block_rows * width
    stat = call(
        functools.partial(stats_kernel, scale, cap, columns, groups),
        jax.ShapeDtypeStruct((8, rows), jnp.float32),
        [
            pltpu.VMEM((slots, rows, block_rows), jnp.float32),
            pltpu.VMEM((rows, block_rows), jnp.float32),
        ],
        flops,
        [me, my_entry],
        [queries, row_weight, positives, near_blocks, *far_blocks],
    )
    pair = jnp.stack([stat, swap(stat, "dp", 1)])
    near_stats = [pair] + [swap(pair, "dp", mask) for mask in range(2, columns, 2)]
    far_stats = [swap(stat, "group", mask) for mask in range(1, groups)]
    grad_query = call(
        functools.partial(query_kernel, scale, cap, columns, groups),
        jax.ShapeDtypeStruct(queries.shape, queries.dtype),
        [
            pltpu.VMEM((rows, width), jnp.float32),
            pltpu.VMEM((rows, cap * block_rows), jnp.bfloat16),
        ],
        2 * flops,
        [me, my_entry],
        [queries, stat, near_blocks, *far_blocks],
    )
    grad_passage = call(
        functools.partial(passage_kernel, scale, cap, near_cap, far_cap, columns, groups),
        jax.ShapeDtypeStruct(passages.shape, passages.dtype),
        [pltpu.VMEM(passages.shape, jnp.float32)],
        2 * flops,
        [me, asked_block, asked_entry],
        [passages, even, odd, *far_queries, *near_stats, *far_stats],
    )
    return (grad_query, grad_passage)


def solution(mesh):
    return jax.shard_map(
        shards,
        mesh=mesh,
        in_specs=(
            P(("group", "dp"), None, None),
            P(("group", "dp"), None, None),
            P(),
            P(("group", "dp"), None),
            P(("group", "dp"), None),
            P(),
        ),
        out_specs=(P(("group", "dp"), None, None), P(("group", "dp"), None, None)),
        check_vma=False,
    )
```

```python
import functools
import math

import jax
import jax.numpy as jnp
from jax import lax
from jax.experimental import pallas as pl
from jax.experimental.pallas import tpu as pltpu
from jax.sharding import PartitionSpec as P

NLOCAL = 12
VMEM_BYTES = 32 * 1024 * 1024
PLAN_VMEM_BYTES = 60 * 1024 * 1024
PLAN_BYTES = 16 * 1024 * 1024
NEAR_BYTES = 64 * 1024 * 1024


def swap(x, axis, mask):
    size = lax.axis_size(axis)
    return lax.ppermute(x, axis, [(i, i ^ mask) for i in range(size)])


def local_call(kernel, tables, inputs, outs, scratch, cost):
    smem = pl.BlockSpec(memory_space=pltpu.SMEM)
    vmem = pl.BlockSpec(memory_space=pltpu.VMEM)
    return pl.pallas_call(
        kernel,
        out_shape=outs,
        in_specs=[smem] * len(tables) + [vmem] * len(inputs),
        out_specs=jax.tree.map(lambda _: vmem, outs),
        scratch_shapes=scratch,
        compiler_params=pltpu.CompilerParams(vmem_limit_bytes=VMEM_BYTES),
        cost_estimate=pl.CostEstimate(flops=0, bytes_accessed=cost, transcendentals=0),
    )(*tables, *inputs)


def start_all(pairs, sems):
    copies = [
        pltpu.make_async_copy(source, target, sems.at[index])
        for index, (source, target) in enumerate(pairs)
    ]
    for copy in copies:
        copy.start()
    return copies


def owners_of(columns, groups):
    group, column = lax.axis_index("group"), lax.axis_index("dp")
    near = [group * columns + (column ^ mask) for mask in range(columns)]
    far = [(group ^ mask) * columns + column for mask in range(1, groups)]
    return near, far


def slot_rows(listings, cap, devices_of):
    query_blocks = len(listings[0])
    shape = listings[0][0].shape
    held = [jnp.zeros(shape, jnp.float32) for _ in range(cap)]
    entry = [jnp.full(shape, -1.0, jnp.float32) for _ in range(query_blocks * cap)]
    rank = jnp.zeros(shape, jnp.float32)
    for index, listing in enumerate(listings):
        listed = devices_of(functools.reduce(jnp.maximum, listing) >= 0.0)
        for slot in range(cap):
            here = listed & (rank == slot)
            held[slot] = jnp.where(here, float(index), held[slot])
            for block in range(query_blocks):
                at = block * cap + slot
                entry[at] = jnp.where(here, listing[block], entry[at])
        rank = rank + jnp.where(listed, 1.0, 0.0)
    return held + entry


def write_rows(rows, out):
    out[...] = jnp.zeros_like(out)
    for index, row in enumerate(rows):
        out[index : index + 1] = row.astype(jnp.int32)


def plan_kernel(scale, cap, near_cap, far_cap, columns, groups, query_blocks, *refs):
    lists_in, owners_in, weight_in, positives_in, passages_in = refs[:5]
    fars, (near_out, asked, wanted, row_data) = refs[5 : 4 + groups], refs[4 + groups : 8 + groups]
    lists, owners, weight, positives, passages, scalars, sems, out_sems, scalar_sem = refs[8 + groups :]
    loads = start_all(
        (
            (lists_in, lists),
            (owners_in, owners),
            (passages_in, passages),
            (weight_in, weight),
            (positives_in, positives),
        ),
        sems,
    )
    devices = columns * groups
    blocks = passages.shape[0]
    listed, lanes = lists.shape
    group, column = lax.axis_index("group"), lax.axis_index("dp")
    device = group * columns + column
    loads[0].wait()
    loads[1].wait()
    number = lax.broadcasted_iota(jnp.int32, (listed, lanes), 0).astype(jnp.float32)
    ids = lax.broadcasted_iota(jnp.int32, owners.shape, 1)
    listings = []
    for block in range(blocks):
        here = owners[...] == device * blocks + block
        block_id = jnp.max(jnp.where(here, ids, 0).astype(jnp.float32), axis=1, keepdims=True)
        match = lists[...] == block_id.astype(jnp.int32)
        listings.append([jnp.max(jnp.where(match, number, -1.0), axis=0, keepdims=True)])
    lane = lax.broadcasted_iota(jnp.int32, (1, lanes), 1)
    place_in = lax.rem(lane, query_blocks)

    def of_device(flags):
        value = jnp.where(flags, 1.0, 0.0)
        most = value
        for other in range(1, query_blocks):
            ahead = jnp.concatenate([value[:, other:], value[:, :other]], axis=1)
            behind = jnp.concatenate([value[:, -other:], value[:, :-other]], axis=1)
            most = jnp.maximum(most, jnp.where(place_in + other < query_blocks, ahead, 0.0))
            most = jnp.maximum(most, jnp.where(place_in >= other, behind, 0.0))
        return most > 0.0

    write_rows(slot_rows(listings, cap, of_device), asked)
    to_scalars = pltpu.make_async_copy(asked, scalars, scalar_sem)
    to_scalars.start()
    loads[2].wait()
    to_scalars.wait()
    pairs = []
    near, far = owners_of(columns, groups)
    for out, owner in zip(fars, far):
        for slot in range(far_cap):
            pairs.append((passages.at[scalars[slot, owner * query_blocks]], out.at[slot]))
    for peer in range(columns):
        owner = group * columns + peer
        for slot in range(near_cap):
            source = passages.at[scalars[slot, owner * query_blocks]]
            pairs.append((source, near_out.at[peer * near_cap + slot]))
    copies = start_all(pairs, out_sems)
    lane = lax.broadcasted_iota(jnp.int32, (listed, lanes), 1)
    place = lax.broadcasted_iota(jnp.int32, (listed, owners.shape[1]), 1)
    first = lax.broadcasted_iota(jnp.int32, (listed, devices), 1) * blocks
    number = lax.broadcasted_iota(jnp.int32, (listed, devices), 0).astype(jnp.float32)
    positions = []
    for block in range(query_blocks):
        mine = jnp.where(lane == device * query_blocks + block, lists[...], 0)
        mine = jnp.max(mine.astype(jnp.float32), axis=1, keepdims=True).astype(jnp.int32)
        found = jnp.where(place == mine, owners[...], 0).astype(jnp.float32)
        positions.append(jnp.max(found, axis=1, keepdims=True).astype(jnp.int32))
    listings = [
        [
            jnp.max(jnp.where(position == first + block, number, -1.0), axis=0, keepdims=True)
            for position in positions
        ]
        for block in range(blocks)
    ]
    write_rows(slot_rows(listings, cap, lambda flags: flags)[cap:], wanted)
    loads[3].wait()
    loads[4].wait()
    row_data[...] = jnp.zeros_like(row_data)
    block_rows = weight.shape[1]
    for block in range(query_blocks):
        mine = slice(block * block_rows, (block + 1) * block_rows)
        row_data[2:3, mine] = weight[block : block + 1] * scale
        row_data[3:4, mine] = positives[block : block + 1].astype(jnp.float32)
    for copy in copies:
        copy.wait()


def near_pieces(near, columns):
    group = lax.axis_index("group")
    cap = near.shape[0] // columns
    for peer in range(columns):
        piece = near[peer * cap : (peer + 1) * cap].reshape(-1, near.shape[-1])
        yield group * columns + peer, piece


def far_pieces(fars, columns, groups):
    for ref, holder in zip(fars, owners_of(columns, groups)[1]):
        yield holder, ref[...].reshape(-1, ref.shape[-1])


def block_scores(scale, entry, cap, holder, query, piece, block_rows):
    scores = (
        lax.dot_general(query, piece, (((1,), (1,)), ((), ())), preferred_element_type=jnp.float32)
        * scale
    )
    for block in range(query.shape[0] // block_rows):
        for slot in range(piece.shape[0] // block_rows):
            listing = entry[block * cap + slot, holder]
            bias = jnp.where(listing >= 0, 0.0, -jnp.inf).astype(jnp.float32)
            rows = slice(block * block_rows, (block + 1) * block_rows)
            columns = slice(slot * block_rows, (slot + 1) * block_rows)
            yield block, slot, listing, scores[rows, columns] + bias


def peak_and_total(scale, entry, cap, queries, pieces, scores_ref, peak_ref):
    query_blocks, block_rows, width = queries.shape
    rows = query_blocks * block_rows
    query = queries[...].reshape(rows, width)
    peak_ref[...] = jnp.full_like(peak_ref, -jnp.inf)
    at = 0
    for holder, piece in pieces:
        for block, slot, _, part in block_scores(
            scale, entry, cap, holder, query, piece, block_rows
        ):
            mine = slice(block * block_rows, (block + 1) * block_rows)
            scores_ref[at + slot, mine] = part
            peak_ref[mine] = jnp.maximum(peak_ref[mine], part)
        at += piece.shape[0] // block_rows
    peak = jnp.max(peak_ref[...], axis=1, keepdims=True)
    total = jnp.zeros((rows, block_rows), jnp.float32)
    for index in range(at):
        total = total + jnp.exp(scores_ref[index] - peak)
    return peak, jnp.sum(total, axis=1, keepdims=True)


def near_kernel(scale, cap, columns, wanted, queries, near, out, scores_ref, peak_ref):
    pieces = near_pieces(near, columns)
    peak, total = peak_and_total(scale, wanted, cap, queries, pieces, scores_ref, peak_ref)
    lane = lax.broadcasted_iota(jnp.int32, out.shape, 1)
    out[...] = jnp.where(lane == 0, peak, total)


def stats_kernel(scale, cap, columns, groups, wanted, queries, row_data, near_stat, *refs):
    fars, (stat, scores_ref, peak_ref) = refs[: groups - 1], refs[groups - 1 :]
    pieces = far_pieces(fars, columns, groups)
    far_peak, far_total = peak_and_total(
        scale, wanted, cap, queries, pieces, scores_ref, peak_ref
    )
    near_peak, near_total = near_stat[:, 0:1], near_stat[:, 1:2]
    peak = jnp.maximum(near_peak, far_peak)
    total = near_total * jnp.exp(near_peak - peak) + far_total * jnp.exp(far_peak - peak)
    lane = lax.broadcasted_iota(jnp.int32, (peak.shape[0], 128), 1)
    turned = jnp.where(lane == 0, peak, total).T
    stat[...] = row_data[...]
    stat[0:2] = turned[0:2]


def query_kernel(scale, cap, columns, groups, wanted, queries, stat, near, *refs):
    fars, (out, total, dscore_ref) = refs[: groups - 1], refs[groups - 1 :]
    query_blocks, block_rows, width = queries.shape
    rows = query_blocks * block_rows
    query = queries[...].reshape(rows, width)
    turned = jnp.concatenate(
        [stat[...], jnp.zeros((128 - stat.shape[0], rows), jnp.float32)], axis=0
    ).T
    peak, inverse = turned[:, 0:1], 1.0 / turned[:, 1:2]
    weight, positive = turned[:, 2:3], turned[:, 3:4]
    place = lax.broadcasted_iota(jnp.int32, (block_rows, block_rows), 1)
    total[...] = jnp.zeros_like(total)
    pieces = list(near_pieces(near, columns)) + list(far_pieces(fars, columns, groups))
    for holder, piece in pieces:
        for block, slot, listing, part in block_scores(
            scale, wanted, cap, holder, query, piece, block_rows
        ):
            mine = slice(block * block_rows, (block + 1) * block_rows)
            number = (place + listing * block_rows).astype(jnp.float32)
            target = jnp.where(positive[mine] == number, 1.0, 0.0)
            chance = jnp.exp(part - peak[mine]) * inverse[mine]
            dscore_ref[mine, slot * block_rows : (slot + 1) * block_rows] = (
                (chance - target) * weight[mine]
            ).astype(jnp.bfloat16)
        total[...] += jnp.dot(
            dscore_ref[:, : piece.shape[0]], piece, preferred_element_type=jnp.float32
        )
    out[...] = total[...].reshape(out.shape).astype(out.dtype)


def passage_kernel(scale, cap, near_cap, far_cap, columns, groups, unit_of, counts, *refs):
    asked, passages = refs[:2]
    query_count, stat_count = counts
    queries_in = refs[2 : 2 + query_count]
    stats_in = refs[2 + query_count : 2 + query_count + stat_count]
    out, total = refs[2 + query_count + stat_count :]
    near, far = owners_of(columns, groups)
    units = [(owner, near_cap) for owner in near] + [(owner, far_cap) for owner in far]
    query_blocks, block_rows, width = queries_in[0].shape
    rows = query_blocks * block_rows
    total[...] = jnp.zeros_like(total)
    lane = lax.broadcasted_iota(jnp.int32, (1, rows), 1)
    place = lax.broadcasted_iota(jnp.int32, (block_rows, rows), 0)
    for unit, (owner, slots) in enumerate(units):
        query, stat = unit_of(unit, queries_in, stats_in)
        query = query[...].reshape(rows, width)
        peak, inverse = stat[0:1], 1.0 / stat[1:2]
        weight, positive = stat[2:3], stat[3:4]
        held = [asked[slot, owner * query_blocks] for slot in range(slots)]
        mine = jnp.concatenate([passages[index] for index in held], axis=0)
        scores = (
            lax.dot_general(
                mine, query, (((1,), (1,)), ((), ())), preferred_element_type=jnp.float32
            )
            * scale
        )
        parts = []
        for slot in range(slots):
            listing = jnp.full((1, rows), asked[cap + slot, owner * query_blocks], jnp.int32)
            for block in range(1, query_blocks):
                later = asked[cap + slot, owner * query_blocks + block]
                listing = jnp.where(lane >= block * block_rows, later, listing)
            bias = jnp.where(listing >= 0, 0.0, -jnp.inf)
            number = (place + listing * block_rows).astype(jnp.float32)
            part = scores[slot * block_rows : (slot + 1) * block_rows] + bias
            target = jnp.where(positive == number, 1.0, 0.0)
            chance = jnp.exp(part - peak) * inverse
            parts.append(((chance - target) * weight).astype(jnp.bfloat16))
        term = jnp.dot(
            jnp.concatenate(parts, axis=0), query, preferred_element_type=jnp.float32
        ).astype(jnp.bfloat16)
        for slot, index in enumerate(held):
            total[index] += term[slot * block_rows : (slot + 1) * block_rows].astype(jnp.float32)
    out[...] = total[...].astype(out.dtype)


def shards(queries, passages, candidates, positives, row_weight, owner_map):
    columns = lax.axis_size("dp")
    groups = lax.axis_size("group")
    devices = columns * groups
    query_blocks, block_rows, width = queries.shape
    rows = query_blocks * block_rows
    blocks = passages.shape[0]
    listed = candidates.shape[1]
    near_cap = (NLOCAL + columns - 1) // columns
    far_cap = (listed - NLOCAL + groups - 2) // (groups - 1)
    cap = max(near_cap, far_cap)
    scale = 3.0 / math.sqrt(width)
    dtype = passages.dtype
    slots = columns * near_cap + (groups - 1) * far_cap
    table_rows = -(-(1 + query_blocks) * cap // 8) * 8
    all_lists = devices * query_blocks

    far_queries = {0: queries}
    far_queries[groups - 1] = swap(queries, "group", groups - 1)
    mask = groups // 2 - 1
    if mask:
        far_queries[mask] = swap(queries, "group", mask)
    near_queries = [queries] + [swap(queries, "dp", mask) for mask in range(2, columns, 2)]

    vmem = pl.BlockSpec(memory_space=pltpu.VMEM)
    hbm = pl.BlockSpec(memory_space=pltpu.HBM)
    far_shape = jax.ShapeDtypeStruct((far_cap, block_rows, width), dtype)
    *far_out, near_out, asked, wanted, row_data = pl.pallas_call(
        functools.partial(
            plan_kernel, scale, cap, near_cap, far_cap, columns, groups, query_blocks
        ),
        out_shape=[far_shape] * (groups - 1)
        + [
            jax.ShapeDtypeStruct((columns * near_cap, block_rows, width), dtype),
            jax.ShapeDtypeStruct((table_rows, all_lists), jnp.int32),
            jax.ShapeDtypeStruct((table_rows, devices), jnp.int32),
            jax.ShapeDtypeStruct((8, rows), jnp.float32),
        ],
        in_specs=[hbm] * 5,
        out_specs=[hbm] * groups + [vmem] * 3,
        scratch_shapes=[
            pltpu.VMEM((listed, all_lists), jnp.int32),
            pltpu.VMEM((1, owner_map.shape[0]), jnp.int32),
            pltpu.VMEM(row_weight.shape, jnp.float32),
            pltpu.VMEM(positives.shape, jnp.int32),
            pltpu.VMEM(passages.shape, dtype),
            pltpu.SMEM((table_rows, all_lists), jnp.int32),
            pltpu.SemaphoreType.DMA((5,)),
            pltpu.SemaphoreType.DMA((slots,)),
            pltpu.SemaphoreType.DMA,
        ],
        compiler_params=pltpu.CompilerParams(vmem_limit_bytes=PLAN_VMEM_BYTES),
        cost_estimate=pl.CostEstimate(flops=0, bytes_accessed=PLAN_BYTES, transcendentals=0),
    )(candidates.T, owner_map.reshape(1, -1), row_weight, positives, passages)
    far_out, near_out, near_queries, far_queries = lax.optimization_barrier(
        (far_out, near_out, near_queries, far_queries)
    )
    far_blocks = [swap(far_out[mask - 1], "group", mask) for mask in range(1, groups)]
    near_blocks = lax.all_to_all(near_out, "dp", split_axis=0, concat_axis=0, tiled=True)
    mask = groups // 2 - 1
    while mask:
        for at, piece in list(far_queries.items()):
            if at ^ mask not in far_queries:
                far_queries[at ^ mask] = swap(piece, "group", mask)
        mask >>= 1
    beside = swap(jnp.concatenate(near_queries), "dp", 1)

    near_slots, far_slots = columns * near_cap, (groups - 1) * far_cap
    near_stat = local_call(
        functools.partial(near_kernel, scale, cap, columns),
        [wanted],
        [queries, near_blocks],
        jax.ShapeDtypeStruct((rows, 128), jnp.float32),
        [
            pltpu.VMEM((near_slots, rows, block_rows), jnp.float32),
            pltpu.VMEM((rows, block_rows), jnp.float32),
        ],
        NEAR_BYTES,
    )
    stat = local_call(
        functools.partial(stats_kernel, scale, cap, columns, groups),
        [wanted],
        [queries, row_data, near_stat, *far_blocks],
        jax.ShapeDtypeStruct((8, rows), jnp.float32),
        [
            pltpu.VMEM((far_slots, rows, block_rows), jnp.float32),
            pltpu.VMEM((rows, block_rows), jnp.float32),
        ],
        0,
    )
    pair = jnp.stack([stat, swap(stat, "dp", 1)])
    near_stats = [pair] + [swap(pair, "dp", mask) for mask in range(2, columns, 2)]
    far_stats = [swap(stat, "group", mask) for mask in range(1, groups)]
    grad_query = local_call(
        functools.partial(query_kernel, scale, cap, columns, groups),
        [wanted],
        [queries, stat, near_blocks, *far_blocks],
        jax.ShapeDtypeStruct(queries.shape, dtype),
        [
            pltpu.VMEM((rows, width), jnp.float32),
            pltpu.VMEM((rows, cap * block_rows), dtype),
        ],
        2 * VMEM_BYTES,
    )

    query_inputs = near_queries + [beside] + [far_queries[mask] for mask in range(1, groups)]
    stat_inputs = near_stats + far_stats

    def unit_of(unit, queries_in, stats_in):
        pairs = columns // 2
        if unit >= columns:
            far = unit - columns
            return queries_in[pairs + 1 + far], stats_in[pairs + far]
        stat = stats_in[unit // 2].at[unit % 2]
        if unit % 2 == 0:
            return queries_in[unit // 2], stat
        return queries_in[pairs].at[pl.ds(unit // 2 * query_blocks, query_blocks)], stat

    grad_passage = local_call(
        functools.partial(
            passage_kernel,
            scale,
            cap,
            near_cap,
            far_cap,
            columns,
            groups,
            unit_of,
            (len(query_inputs), len(stat_inputs)),
        ),
        [asked],
        [passages, *query_inputs, *stat_inputs],
        jax.ShapeDtypeStruct(passages.shape, dtype),
        [pltpu.VMEM(passages.shape, jnp.float32)],
        0,
    )
    return (grad_query, grad_passage)


def solution(mesh):
    return jax.shard_map(
        shards,
        mesh=mesh,
        in_specs=(
            P(("group", "dp"), None, None),
            P(("group", "dp"), None, None),
            P(),
            P(("group", "dp"), None),
            P(("group", "dp"), None),
            P(),
        ),
        out_specs=(P(("group", "dp"), None, None), P(("group", "dp"), None, None)),
        check_vma=False,
    )
```

```python
import functools
import math

import jax
import jax.numpy as jnp
from jax import lax
from jax.experimental import pallas as pl
from jax.experimental.pallas import tpu as pltpu
from jax.sharding import PartitionSpec as P

NLOCAL = 12
VMEM_BYTES = 32 * 1024 * 1024
PLAN_VMEM_BYTES = 63 * 1024 * 1024
PLAN_BYTES = 16 * 1024 * 1024
NEAR_BYTES = 64 * 1024 * 1024


def swap(x, axis, mask):
    size = lax.axis_size(axis)
    return lax.ppermute(x, axis, [(i, i ^ mask) for i in range(size)])


def local_call(kernel, tables, inputs, outs, scratch, cost):
    smem = pl.BlockSpec(memory_space=pltpu.SMEM)
    vmem = pl.BlockSpec(memory_space=pltpu.VMEM)
    return pl.pallas_call(
        kernel,
        out_shape=outs,
        in_specs=[smem] * len(tables) + [vmem] * len(inputs),
        out_specs=jax.tree.map(lambda _: vmem, outs),
        scratch_shapes=scratch,
        compiler_params=pltpu.CompilerParams(vmem_limit_bytes=VMEM_BYTES),
        cost_estimate=pl.CostEstimate(flops=0, bytes_accessed=cost, transcendentals=0),
    )(*tables, *inputs)


def start_all(pairs, sems):
    copies = [
        pltpu.make_async_copy(source, target, sems.at[index])
        for index, (source, target) in enumerate(pairs)
    ]
    for copy in copies:
        copy.start()
    return copies


def owners_of(columns, groups):
    group, column = lax.axis_index("group"), lax.axis_index("dp")
    near = [group * columns + (column ^ mask) for mask in range(columns)]
    far = [(group ^ mask) * columns + column for mask in range(1, groups)]
    return near, far


def slot_rows(listings, cap, devices_of):
    query_blocks = len(listings[0])
    shape = listings[0][0].shape
    held = [jnp.zeros(shape, jnp.float32) for _ in range(cap)]
    entry = [jnp.full(shape, -1.0, jnp.float32) for _ in range(query_blocks * cap)]
    rank = jnp.zeros(shape, jnp.float32)
    for index, listing in enumerate(listings):
        listed = devices_of(functools.reduce(jnp.maximum, listing) >= 0.0)
        for slot in range(cap):
            here = listed & (rank == slot)
            held[slot] = jnp.where(here, float(index), held[slot])
            for block in range(query_blocks):
                at = block * cap + slot
                entry[at] = jnp.where(here, listing[block], entry[at])
        rank = rank + jnp.where(listed, 1.0, 0.0)
    return held + entry


def write_rows(rows, out):
    out[...] = jnp.zeros_like(out)
    for index, row in enumerate(rows):
        out[index : index + 1] = row.astype(jnp.int32)


def plan_kernel(scale, cap, near_cap, far_cap, columns, groups, query_blocks, *refs):
    lists_in, owners_in, weight_in, positives_in, passages_in = refs[:5]
    fars, (near_out, asked, numbers, row_data) = refs[5 : 4 + groups], refs[4 + groups : 8 + groups]
    lists, owners, weight, positives, passages, wanted = refs[8 + groups : 14 + groups]
    scalars, wanted_scalars, sems, out_sems, scalar_sems = refs[14 + groups :]
    loads = start_all(
        (
            (lists_in, lists),
            (owners_in, owners),
            (passages_in, passages),
            (weight_in, weight),
            (positives_in, positives),
        ),
        sems,
    )
    devices = columns * groups
    blocks = passages.shape[0]
    listed, lanes = lists.shape
    group, column = lax.axis_index("group"), lax.axis_index("dp")
    device = group * columns + column
    loads[0].wait()
    loads[1].wait()
    number = lax.broadcasted_iota(jnp.int32, (listed, lanes), 0).astype(jnp.float32)
    ids = lax.broadcasted_iota(jnp.int32, owners.shape, 1)
    listings = []
    for block in range(blocks):
        here = owners[...] == device * blocks + block
        block_id = jnp.max(jnp.where(here, ids, 0).astype(jnp.float32), axis=1, keepdims=True)
        match = lists[...] == block_id.astype(jnp.int32)
        listings.append([jnp.max(jnp.where(match, number, -1.0), axis=0, keepdims=True)])
    lane = lax.broadcasted_iota(jnp.int32, (1, lanes), 1)
    place_in = lax.rem(lane, query_blocks)

    def of_device(flags):
        value = jnp.where(flags, 1.0, 0.0)
        most = value
        for other in range(1, query_blocks):
            ahead = jnp.concatenate([value[:, other:], value[:, :other]], axis=1)
            behind = jnp.concatenate([value[:, -other:], value[:, :-other]], axis=1)
            most = jnp.maximum(most, jnp.where(place_in + other < query_blocks, ahead, 0.0))
            most = jnp.maximum(most, jnp.where(place_in >= other, behind, 0.0))
        return most > 0.0

    write_rows(slot_rows(listings, cap, of_device), asked)
    to_scalars = pltpu.make_async_copy(asked, scalars, scalar_sems.at[0])
    to_scalars.start()
    loads[2].wait()
    to_scalars.wait()
    pairs = []
    near, far = owners_of(columns, groups)
    for out, owner in zip(fars, far):
        for slot in range(far_cap):
            pairs.append((passages.at[scalars[slot, owner * query_blocks]], out.at[slot]))
    for peer in range(columns):
        owner = group * columns + peer
        for slot in range(near_cap):
            source = passages.at[scalars[slot, owner * query_blocks]]
            pairs.append((source, near_out.at[peer * near_cap + slot]))
    copies = start_all(pairs, out_sems)
    lane = lax.broadcasted_iota(jnp.int32, (listed, lanes), 1)
    place = lax.broadcasted_iota(jnp.int32, (listed, owners.shape[1]), 1)
    first = lax.broadcasted_iota(jnp.int32, (listed, devices), 1) * blocks
    number = lax.broadcasted_iota(jnp.int32, (listed, devices), 0).astype(jnp.float32)
    positions = []
    for block in range(query_blocks):
        mine = jnp.where(lane == device * query_blocks + block, lists[...], 0)
        mine = jnp.max(mine.astype(jnp.float32), axis=1, keepdims=True).astype(jnp.int32)
        found = jnp.where(place == mine, owners[...], 0).astype(jnp.float32)
        positions.append(jnp.max(found, axis=1, keepdims=True).astype(jnp.int32))
    listings = [
        [
            jnp.max(jnp.where(position == first + block, number, -1.0), axis=0, keepdims=True)
            for position in positions
        ]
        for block in range(blocks)
    ]
    write_rows(slot_rows(listings, cap, lambda flags: flags)[cap:], wanted)
    to_scalars = pltpu.make_async_copy(wanted, wanted_scalars, scalar_sems.at[1])
    to_scalars.start()
    loads[3].wait()
    loads[4].wait()
    row_data[...] = jnp.zeros_like(row_data)
    block_rows = weight.shape[1]
    for block in range(query_blocks):
        mine = slice(block * block_rows, (block + 1) * block_rows)
        row_data[2:3, mine] = weight[block : block + 1] * scale
        row_data[3:4, mine] = positives[block : block + 1].astype(jnp.float32)
    to_scalars.wait()
    numbers[...] = jnp.full_like(numbers, -1.0)
    place = lax.broadcasted_iota(jnp.int32, (1, block_rows), 1)
    entries = [(group * columns + peer, slot) for peer in range(columns) for slot in range(near_cap)]
    entries += [(owner, slot) for owner in far for slot in range(far_cap)]
    for index, (owner, slot) in enumerate(entries):
        for block in range(query_blocks):
            listing = wanted_scalars[block * cap + slot, owner]
            number = jnp.where(listing >= 0, place + listing * block_rows, -1)
            numbers[block : block + 1, index * block_rows : (index + 1) * block_rows] = (
                number.astype(jnp.float32)
            )
    for copy in copies:
        copy.wait()


def score_blocks(scale, queries, pieces, numbers, first, scores, peak_ref):
    query_blocks, block_rows, width = queries.shape
    rows = query_blocks * block_rows
    query = queries[...].reshape(rows, width)
    peak_ref[...] = jnp.full_like(peak_ref, -jnp.inf)
    at = 0
    for piece in pieces:
        size = piece.shape[0]
        part = lax.dot_general(
            query, piece, (((1,), (1,)), ((), ())), preferred_element_type=jnp.float32
        )
        for block in range(query_blocks):
            mine = slice(block * block_rows, (block + 1) * block_rows)
            number = numbers[block : block + 1, first + at : first + at + size]
            own = jnp.where(number >= 0.0, part[mine] * scale, -jnp.inf)
            scores[mine, at : at + size] = own
            peak = peak_ref[mine]
            for column in range(0, size, block_rows):
                peak = jnp.maximum(peak, own[:, column : column + block_rows])
            peak_ref[mine] = peak
        at += size
    peak = jnp.max(peak_ref[...], axis=1, keepdims=True)
    total = jnp.zeros((rows, block_rows), jnp.float32)
    for column in range(0, at, block_rows):
        total = total + jnp.exp(scores[:, column : column + block_rows] - peak)
    return peak, jnp.sum(total, axis=1, keepdims=True)


def near_pieces(near, columns):
    cap = near.shape[0] // columns
    for peer in range(columns):
        yield near[peer * cap : (peer + 1) * cap].reshape(-1, near.shape[-1])


def far_pieces(fars):
    for ref in fars:
        yield ref[...].reshape(-1, ref.shape[-1])


def near_kernel(scale, columns, queries, numbers, near, out, scores, peak_ref):
    pieces = near_pieces(near, columns)
    peak, total = score_blocks(scale, queries, pieces, numbers, 0, scores, peak_ref)
    lane = lax.broadcasted_iota(jnp.int32, out.shape, 1)
    out[...] = jnp.where(lane == 0, peak, total)


def stats_kernel(scale, first, queries, row_data, numbers, near_stat, *refs):
    fars, (stat, scores, peak_ref) = refs[:-3], refs[-3:]
    far_peak, far_total = score_blocks(
        scale, queries, far_pieces(fars), numbers, first, scores, peak_ref
    )
    near_peak, near_total = near_stat[:, 0:1], near_stat[:, 1:2]
    peak = jnp.maximum(near_peak, far_peak)
    total = near_total * jnp.exp(near_peak - peak) + far_total * jnp.exp(far_peak - peak)
    lane = lax.broadcasted_iota(jnp.int32, (peak.shape[0], 128), 1)
    turned = jnp.where(lane == 0, peak, total).T
    stat[...] = row_data[...]
    stat[0:2] = turned[0:2]


def query_kernel(columns, numbers, stat, near_scores, far_scores, near, *refs):
    fars, (out, total, dscore_ref) = refs[:-3], refs[-3:]
    query_blocks, block_rows, width = out.shape
    rows = query_blocks * block_rows
    turned = jnp.concatenate(
        [stat[...], jnp.zeros((128 - stat.shape[0], rows), jnp.float32)], axis=0
    ).T
    peak, inverse = turned[:, 0:1], 1.0 / turned[:, 1:2]
    weight, positive = turned[:, 2:3], turned[:, 3:4]
    total[...] = jnp.zeros_like(total)
    first = 0
    for scores, pieces in ((near_scores, near_pieces(near, columns)), (far_scores, far_pieces(fars))):
        at = 0
        for piece in pieces:
            size = piece.shape[0]
            for block in range(query_blocks):
                mine = slice(block * block_rows, (block + 1) * block_rows)
                number = numbers[block : block + 1, first + at : first + at + size]
                chance = jnp.exp(scores[mine, at : at + size] - peak[mine]) * inverse[mine]
                target = jnp.where(positive[mine] == number, 1.0, 0.0)
                dscore_ref[mine, :size] = ((chance - target) * weight[mine]).astype(jnp.bfloat16)
            total[...] += jnp.dot(
                dscore_ref[:, :size], piece, preferred_element_type=jnp.float32
            )
            at += size
        first += at
    out[...] = total[...].reshape(out.shape).astype(out.dtype)


def passage_kernel(scale, cap, near_cap, far_cap, columns, groups, unit_of, counts, *refs):
    asked, passages = refs[:2]
    query_count, stat_count = counts
    queries_in = refs[2 : 2 + query_count]
    stats_in = refs[2 + query_count : 2 + query_count + stat_count]
    out, total = refs[2 + query_count + stat_count :]
    near, far = owners_of(columns, groups)
    units = [(owner, near_cap) for owner in near] + [(owner, far_cap) for owner in far]
    query_blocks, block_rows, width = queries_in[0].shape
    rows = query_blocks * block_rows
    total[...] = jnp.zeros_like(total)
    lane = lax.broadcasted_iota(jnp.int32, (1, rows), 1)
    place = lax.broadcasted_iota(jnp.int32, (block_rows, rows), 0).astype(jnp.float32)
    for unit, (owner, slots) in enumerate(units):
        query, stat = unit_of(unit, queries_in, stats_in)
        query = query[...].reshape(rows, width)
        peak, weight, positive = stat[0:1], stat[2:3], stat[3:4]
        share = weight / stat[1:2]
        held = [asked[slot, owner * query_blocks] for slot in range(slots)]
        mine = jnp.concatenate([passages[index] for index in held], axis=0)
        scores = (
            lax.dot_general(
                mine, query, (((1,), (1,)), ((), ())), preferred_element_type=jnp.float32
            )
            * scale
        )
        parts = []
        for slot in range(slots):
            listing = jnp.full((1, rows), asked[cap + slot, owner * query_blocks], jnp.int32)
            for block in range(1, query_blocks):
                later = asked[cap + slot, owner * query_blocks + block]
                listing = jnp.where(lane >= block * block_rows, later, listing)
            bias = jnp.where(listing >= 0, -peak, -jnp.inf)
            row = positive - (listing * block_rows).astype(jnp.float32)
            part = scores[slot * block_rows : (slot + 1) * block_rows]
            target = jnp.where(row == place, weight, 0.0)
            parts.append((jnp.exp(part + bias) * share - target).astype(jnp.bfloat16))
        term = jnp.dot(
            jnp.concatenate(parts, axis=0), query, preferred_element_type=jnp.float32
        ).astype(jnp.bfloat16)
        for slot, index in enumerate(held):
            total[index] += term[slot * block_rows : (slot + 1) * block_rows].astype(jnp.float32)
    out[...] = total[...].astype(out.dtype)


def shards(queries, passages, candidates, positives, row_weight, owner_map):
    columns = lax.axis_size("dp")
    groups = lax.axis_size("group")
    devices = columns * groups
    query_blocks, block_rows, width = queries.shape
    rows = query_blocks * block_rows
    blocks = passages.shape[0]
    listed = candidates.shape[1]
    near_cap = (NLOCAL + columns - 1) // columns
    far_cap = (listed - NLOCAL + groups - 2) // (groups - 1)
    cap = max(near_cap, far_cap)
    scale = 3.0 / math.sqrt(width)
    dtype = passages.dtype
    slots = columns * near_cap + (groups - 1) * far_cap
    table_rows = -(-(1 + query_blocks) * cap // 8) * 8
    all_lists = devices * query_blocks

    far_queries = {0: queries}
    far_queries[groups - 1] = swap(queries, "group", groups - 1)
    mask = groups // 2 - 1
    if mask:
        far_queries[mask] = swap(queries, "group", mask)
    near_queries = [queries] + [swap(queries, "dp", mask) for mask in range(2, columns, 2)]

    vmem = pl.BlockSpec(memory_space=pltpu.VMEM)
    hbm = pl.BlockSpec(memory_space=pltpu.HBM)
    far_shape = jax.ShapeDtypeStruct((far_cap, block_rows, width), dtype)
    *far_out, near_out, asked, numbers, row_data = pl.pallas_call(
        functools.partial(
            plan_kernel, scale, cap, near_cap, far_cap, columns, groups, query_blocks
        ),
        out_shape=[far_shape] * (groups - 1)
        + [
            jax.ShapeDtypeStruct((columns * near_cap, block_rows, width), dtype),
            jax.ShapeDtypeStruct((table_rows, all_lists), jnp.int32),
            jax.ShapeDtypeStruct((8, slots * block_rows), jnp.float32),
            jax.ShapeDtypeStruct((8, rows), jnp.float32),
        ],
        in_specs=[hbm] * 5,
        out_specs=[hbm] * groups + [vmem] * 3,
        scratch_shapes=[
            pltpu.VMEM((listed, all_lists), jnp.int32),
            pltpu.VMEM((1, owner_map.shape[0]), jnp.int32),
            pltpu.VMEM(row_weight.shape, jnp.float32),
            pltpu.VMEM(positives.shape, jnp.int32),
            pltpu.VMEM(passages.shape, dtype),
            pltpu.VMEM((table_rows, devices), jnp.int32),
            pltpu.SMEM((table_rows, all_lists), jnp.int32),
            pltpu.SMEM((table_rows, devices), jnp.int32),
            pltpu.SemaphoreType.DMA((5,)),
            pltpu.SemaphoreType.DMA((slots,)),
            pltpu.SemaphoreType.DMA((2,)),
        ],
        compiler_params=pltpu.CompilerParams(vmem_limit_bytes=PLAN_VMEM_BYTES),
        cost_estimate=pl.CostEstimate(flops=0, bytes_accessed=PLAN_BYTES, transcendentals=0),
    )(candidates.T, owner_map.reshape(1, -1), row_weight, positives, passages)
    far_out, near_out, near_queries, far_queries = lax.optimization_barrier(
        (far_out, near_out, near_queries, far_queries)
    )
    far_blocks = [swap(far_out[mask - 1], "group", mask) for mask in range(1, groups)]
    near_blocks = lax.all_to_all(near_out, "dp", split_axis=0, concat_axis=0, tiled=True)
    mask = groups // 2 - 1
    while mask:
        for at, piece in list(far_queries.items()):
            if at ^ mask not in far_queries:
                far_queries[at ^ mask] = swap(piece, "group", mask)
        mask >>= 1
    beside = swap(jnp.concatenate(near_queries), "dp", 1)

    near_slots, far_slots = columns * near_cap, (groups - 1) * far_cap
    near_stat, near_scores = local_call(
        functools.partial(near_kernel, scale, columns),
        [],
        [queries, numbers, near_blocks],
        [
            jax.ShapeDtypeStruct((rows, 128), jnp.float32),
            jax.ShapeDtypeStruct((rows, near_slots * block_rows), jnp.float32),
        ],
        [pltpu.VMEM((rows, block_rows), jnp.float32)],
        NEAR_BYTES,
    )
    stat, far_scores = local_call(
        functools.partial(stats_kernel, scale, near_slots * block_rows),
        [],
        [queries, row_data, numbers, near_stat, *far_blocks],
        [
            jax.ShapeDtypeStruct((8, rows), jnp.float32),
            jax.ShapeDtypeStruct((rows, far_slots * block_rows), jnp.float32),
        ],
        [pltpu.VMEM((rows, block_rows), jnp.float32)],
        0,
    )
    pair = jnp.stack([stat, swap(stat, "dp", 1)])
    near_stats = [pair] + [swap(pair, "dp", mask) for mask in range(2, columns, 2)]
    far_pair = jnp.stack([stat, swap(stat, "group", 1)])
    far_stats = [far_pair] + [swap(far_pair, "group", mask) for mask in range(2, groups, 2)]
    grad_query = local_call(
        functools.partial(query_kernel, columns),
        [],
        [numbers, stat, near_scores, far_scores, near_blocks, *far_blocks],
        jax.ShapeDtypeStruct(queries.shape, dtype),
        [
            pltpu.VMEM((rows, width), jnp.float32),
            pltpu.VMEM((rows, cap * block_rows), dtype),
        ],
        2 * VMEM_BYTES,
    )

    query_inputs = near_queries + [beside] + [far_queries[mask] for mask in range(1, groups)]
    stat_inputs = near_stats + far_stats

    def unit_of(unit, queries_in, stats_in):
        pairs = columns // 2
        if unit >= columns:
            far = unit - columns
            place = (far + 1) // 2
            return queries_in[pairs + 1 + far], stats_in[pairs + place].at[(far + 1) % 2]
        stat = stats_in[unit // 2].at[unit % 2]
        if unit % 2 == 0:
            return queries_in[unit // 2], stat
        return queries_in[pairs].at[pl.ds(unit // 2 * query_blocks, query_blocks)], stat

    grad_passage = local_call(
        functools.partial(
            passage_kernel,
            scale,
            cap,
            near_cap,
            far_cap,
            columns,
            groups,
            unit_of,
            (len(query_inputs), len(stat_inputs)),
        ),
        [asked],
        [passages, *query_inputs, *stat_inputs],
        jax.ShapeDtypeStruct(passages.shape, dtype),
        [pltpu.VMEM(passages.shape, jnp.float32)],
        0,
    )
    return (grad_query, grad_passage)


def solution(mesh):
    return jax.shard_map(
        shards,
        mesh=mesh,
        in_specs=(
            P(("group", "dp"), None, None),
            P(("group", "dp"), None, None),
            P(),
            P(("group", "dp"), None),
            P(("group", "dp"), None),
            P(),
        ),
        out_specs=(P(("group", "dp"), None, None), P(("group", "dp"), None, None)),
        check_vma=False,
    )
```

```python
import functools
import math

import jax
import jax.numpy as jnp
from jax import lax
from jax.experimental import pallas as pl
from jax.experimental.pallas import tpu as pltpu
from jax.sharding import PartitionSpec as P

NLOCAL = 12
VMEM_BYTES = 32 * 1024 * 1024
PLAN_VMEM_BYTES = 63 * 1024 * 1024
PLAN_BYTES = 16 * 1024 * 1024
NEAR_BYTES = 64 * 1024 * 1024


def swap(x, axis, mask):
    size = lax.axis_size(axis)
    return lax.ppermute(x, axis, [(i, i ^ mask) for i in range(size)])


def local_call(kernel, tables, inputs, outs, scratch, cost):
    smem = pl.BlockSpec(memory_space=pltpu.SMEM)
    vmem = pl.BlockSpec(memory_space=pltpu.VMEM)
    return pl.pallas_call(
        kernel,
        out_shape=outs,
        in_specs=[smem] * len(tables) + [vmem] * len(inputs),
        out_specs=jax.tree.map(lambda _: vmem, outs),
        scratch_shapes=scratch,
        compiler_params=pltpu.CompilerParams(vmem_limit_bytes=VMEM_BYTES),
        cost_estimate=pl.CostEstimate(flops=0, bytes_accessed=cost, transcendentals=0),
    )(*tables, *inputs)


def start_all(pairs, sems):
    copies = [
        pltpu.make_async_copy(source, target, sems.at[index])
        for index, (source, target) in enumerate(pairs)
    ]
    for copy in copies:
        copy.start()
    return copies


def owners_of(columns, groups):
    group, column = lax.axis_index("group"), lax.axis_index("dp")
    near = [group * columns + (column ^ mask) for mask in range(columns)]
    far = [(group ^ mask) * columns + column for mask in range(1, groups)]
    return near, far


def slot_rows(listings, cap, devices_of):
    query_blocks = len(listings[0])
    shape = listings[0][0].shape
    held = [jnp.zeros(shape, jnp.float32) for _ in range(cap)]
    entry = [jnp.full(shape, -1.0, jnp.float32) for _ in range(query_blocks * cap)]
    rank = jnp.zeros(shape, jnp.float32)
    for index, listing in enumerate(listings):
        listed = devices_of(functools.reduce(jnp.maximum, listing) >= 0.0)
        for slot in range(cap):
            here = listed & (rank == slot)
            held[slot] = jnp.where(here, float(index), held[slot])
            for block in range(query_blocks):
                at = block * cap + slot
                entry[at] = jnp.where(here, listing[block], entry[at])
        rank = rank + jnp.where(listed, 1.0, 0.0)
    return held + entry


def write_rows(rows, out):
    out[...] = jnp.zeros_like(out)
    for index, row in enumerate(rows):
        out[index : index + 1] = row.astype(jnp.int32)


def plan_kernel(scale, cap, near_cap, far_cap, columns, groups, query_blocks, *refs):
    lists_in, owners_in, weight_in, positives_in, passages_in = refs[:5]
    fars, (near_out, asked, numbers, row_data) = refs[5 : 4 + groups], refs[4 + groups : 8 + groups]
    lists, owners, weight, positives, passages, wanted = refs[8 + groups : 14 + groups]
    scalars, wanted_scalars, sems, out_sems, scalar_sems = refs[14 + groups :]
    loads = start_all(
        (
            (lists_in, lists),
            (owners_in, owners),
            (passages_in, passages),
            (weight_in, weight),
            (positives_in, positives),
        ),
        sems,
    )
    devices = columns * groups
    blocks = passages.shape[0]
    listed, lanes = lists.shape
    group, column = lax.axis_index("group"), lax.axis_index("dp")
    device = group * columns + column
    loads[0].wait()
    loads[1].wait()
    number = lax.broadcasted_iota(jnp.int32, (listed, lanes), 0).astype(jnp.float32)
    ids = lax.broadcasted_iota(jnp.int32, owners.shape, 1)
    listings = []
    for block in range(blocks):
        here = owners[...] == device * blocks + block
        block_id = jnp.max(jnp.where(here, ids, 0).astype(jnp.float32), axis=1, keepdims=True)
        match = lists[...] == block_id.astype(jnp.int32)
        listings.append([jnp.max(jnp.where(match, number, -1.0), axis=0, keepdims=True)])
    lane = lax.broadcasted_iota(jnp.int32, (1, lanes), 1)
    place_in = lax.rem(lane, query_blocks)

    def of_device(flags):
        value = jnp.where(flags, 1.0, 0.0)
        most = value
        for other in range(1, query_blocks):
            ahead = jnp.concatenate([value[:, other:], value[:, :other]], axis=1)
            behind = jnp.concatenate([value[:, -other:], value[:, :-other]], axis=1)
            most = jnp.maximum(most, jnp.where(place_in + other < query_blocks, ahead, 0.0))
            most = jnp.maximum(most, jnp.where(place_in >= other, behind, 0.0))
        return most > 0.0

    write_rows(slot_rows(listings, cap, of_device), asked)
    to_scalars = pltpu.make_async_copy(asked, scalars, scalar_sems.at[0])
    to_scalars.start()
    loads[2].wait()
    to_scalars.wait()
    pairs = []
    near, far = owners_of(columns, groups)
    for out, owner in zip(fars, far):
        for slot in range(far_cap):
            pairs.append((passages.at[scalars[slot, owner * query_blocks]], out.at[slot]))
    for peer in range(columns):
        owner = group * columns + peer
        for slot in range(near_cap):
            source = passages.at[scalars[slot, owner * query_blocks]]
            pairs.append((source, near_out.at[peer * near_cap + slot]))
    copies = start_all(pairs, out_sems)
    lane = lax.broadcasted_iota(jnp.int32, (listed, lanes), 1)
    place = lax.broadcasted_iota(jnp.int32, (listed, owners.shape[1]), 1)
    first = lax.broadcasted_iota(jnp.int32, (listed, devices), 1) * blocks
    number = lax.broadcasted_iota(jnp.int32, (listed, devices), 0).astype(jnp.float32)
    positions = []
    for block in range(query_blocks):
        mine = jnp.where(lane == device * query_blocks + block, lists[...], 0)
        mine = jnp.max(mine.astype(jnp.float32), axis=1, keepdims=True).astype(jnp.int32)
        found = jnp.where(place == mine, owners[...], 0).astype(jnp.float32)
        positions.append(jnp.max(found, axis=1, keepdims=True).astype(jnp.int32))
    listings = [
        [
            jnp.max(jnp.where(position == first + block, number, -1.0), axis=0, keepdims=True)
            for position in positions
        ]
        for block in range(blocks)
    ]
    write_rows(slot_rows(listings, cap, lambda flags: flags)[cap:], wanted)
    to_scalars = pltpu.make_async_copy(wanted, wanted_scalars, scalar_sems.at[1])
    to_scalars.start()
    loads[3].wait()
    loads[4].wait()
    row_data[...] = jnp.zeros_like(row_data)
    block_rows = weight.shape[1]
    for block in range(query_blocks):
        mine = slice(block * block_rows, (block + 1) * block_rows)
        row_data[2:3, mine] = weight[block : block + 1] * scale
        row_data[3:4, mine] = positives[block : block + 1].astype(jnp.float32)
    to_scalars.wait()
    numbers[...] = jnp.full_like(numbers, -1.0)
    place = lax.broadcasted_iota(jnp.int32, (1, block_rows), 1)
    entries = [(group * columns + peer, slot) for peer in range(columns) for slot in range(near_cap)]
    entries += [(owner, slot) for owner in far for slot in range(far_cap)]
    for index, (owner, slot) in enumerate(entries):
        for block in range(query_blocks):
            listing = wanted_scalars[block * cap + slot, owner]
            number = jnp.where(listing >= 0, place + listing * block_rows, -1)
            numbers[block : block + 1, index * block_rows : (index + 1) * block_rows] = (
                number.astype(jnp.float32)
            )
    for copy in copies:
        copy.wait()


def score_blocks(scale, queries, pieces, numbers, first, scores, peak_ref):
    query_blocks, block_rows, width = queries.shape
    rows = query_blocks * block_rows
    query = queries[...].reshape(rows, width)
    peak_ref[...] = jnp.full_like(peak_ref, -jnp.inf)
    at = 0
    for piece in pieces:
        size = piece.shape[0]
        part = lax.dot_general(
            query, piece, (((1,), (1,)), ((), ())), preferred_element_type=jnp.float32
        )
        for block in range(query_blocks):
            mine = slice(block * block_rows, (block + 1) * block_rows)
            number = numbers[block : block + 1, first + at : first + at + size]
            own = jnp.where(number >= 0.0, part[mine] * scale, -jnp.inf)
            scores[mine, at : at + size] = own
            peak = peak_ref[mine]
            for column in range(0, size, block_rows):
                peak = jnp.maximum(peak, own[:, column : column + block_rows])
            peak_ref[mine] = peak
        at += size
    peak = jnp.max(peak_ref[...], axis=1, keepdims=True)
    total = jnp.zeros((rows, block_rows), jnp.float32)
    for column in range(0, at, block_rows):
        total = total + jnp.exp(scores[:, column : column + block_rows] - peak)
    return peak, jnp.sum(total, axis=1, keepdims=True)


def near_pieces(near, columns):
    cap = near.shape[0] // columns
    for peer in range(columns):
        yield near[peer * cap : (peer + 1) * cap].reshape(-1, near.shape[-1])


def far_pieces(fars):
    for ref in fars:
        yield ref[...].reshape(-1, ref.shape[-1])


def near_kernel(scale, columns, queries, numbers, near, out, scores, peak_ref):
    pieces = near_pieces(near, columns)
    peak, total = score_blocks(scale, queries, pieces, numbers, 0, scores, peak_ref)
    lane = lax.broadcasted_iota(jnp.int32, out.shape, 1)
    out[...] = jnp.where(lane == 0, peak, total)


def stats_kernel(scale, first, queries, row_data, numbers, near_stat, *refs):
    fars, (stat, scores, peak_ref) = refs[:-3], refs[-3:]
    far_peak, far_total = score_blocks(
        scale, queries, far_pieces(fars), numbers, first, scores, peak_ref
    )
    near_peak, near_total = near_stat[:, 0:1], near_stat[:, 1:2]
    peak = jnp.maximum(near_peak, far_peak)
    total = near_total * jnp.exp(near_peak - peak) + far_total * jnp.exp(far_peak - peak)
    lane = lax.broadcasted_iota(jnp.int32, (peak.shape[0], 128), 1)
    turned = jnp.where(lane == 0, peak, total).T
    stat[...] = row_data[...]
    stat[0:2] = turned[0:2]


def query_kernel(columns, numbers, stat, near_scores, far_scores, near, *refs):
    fars, (out, total, dscore_ref) = refs[:-3], refs[-3:]
    query_blocks, block_rows, width = out.shape
    rows = query_blocks * block_rows
    turned = jnp.concatenate(
        [stat[...], jnp.zeros((128 - stat.shape[0], rows), jnp.float32)], axis=0
    ).T
    peak, inverse = turned[:, 0:1], 1.0 / turned[:, 1:2]
    weight, positive = turned[:, 2:3], turned[:, 3:4]
    total[...] = jnp.zeros_like(total)
    first = 0
    for scores, pieces in ((near_scores, near_pieces(near, columns)), (far_scores, far_pieces(fars))):
        at = 0
        for piece in pieces:
            size = piece.shape[0]
            for block in range(query_blocks):
                mine = slice(block * block_rows, (block + 1) * block_rows)
                number = numbers[block : block + 1, first + at : first + at + size]
                chance = jnp.exp(scores[mine, at : at + size] - peak[mine]) * inverse[mine]
                target = jnp.where(positive[mine] == number, 1.0, 0.0)
                dscore_ref[mine, :size] = ((chance - target) * weight[mine]).astype(jnp.bfloat16)
            total[...] += jnp.dot(
                dscore_ref[:, :size], piece, preferred_element_type=jnp.float32
            )
            at += size
        first += at
    out[...] = total[...].reshape(out.shape).astype(out.dtype)


def passage_kernel(scale, cap, near_cap, far_cap, columns, groups, unit_of, counts, *refs):
    asked, passages = refs[:2]
    query_count, stat_count = counts
    queries_in = refs[2 : 2 + query_count]
    stats_in = refs[2 + query_count : 2 + query_count + stat_count]
    out, total = refs[2 + query_count + stat_count :]
    near, far = owners_of(columns, groups)
    units = [(owner, near_cap) for owner in near] + [(owner, far_cap) for owner in far]
    query_blocks, block_rows, width = queries_in[0].shape
    rows = query_blocks * block_rows
    total[...] = jnp.zeros_like(total)
    lane = lax.broadcasted_iota(jnp.int32, (1, rows), 1)
    place = lax.broadcasted_iota(jnp.int32, (block_rows, rows), 0).astype(jnp.float32)
    for unit, (owner, slots) in enumerate(units):
        query, stat = unit_of(unit, queries_in, stats_in)
        query = query[...].reshape(rows, width)
        peak, weight, positive = stat[0:1], stat[2:3], stat[3:4]
        share = weight / stat[1:2]
        held = [asked[slot, owner * query_blocks] for slot in range(slots)]
        mine = jnp.concatenate([passages[index] for index in held], axis=0)
        scores = (
            lax.dot_general(
                mine, query, (((1,), (1,)), ((), ())), preferred_element_type=jnp.float32
            )
            * scale
        )
        parts = []
        for slot in range(slots):
            listing = jnp.full((1, rows), asked[cap + slot, owner * query_blocks], jnp.int32)
            for block in range(1, query_blocks):
                later = asked[cap + slot, owner * query_blocks + block]
                listing = jnp.where(lane >= block * block_rows, later, listing)
            bias = jnp.where(listing >= 0, -peak, -jnp.inf)
            row = positive - (listing * block_rows).astype(jnp.float32)
            part = scores[slot * block_rows : (slot + 1) * block_rows]
            target = jnp.where(row == place, weight, 0.0)
            parts.append((jnp.exp(part + bias) * share - target).astype(jnp.bfloat16))
        term = jnp.dot(
            jnp.concatenate(parts, axis=0), query, preferred_element_type=jnp.float32
        ).astype(jnp.bfloat16)
        for slot, index in enumerate(held):
            total[index] += term[slot * block_rows : (slot + 1) * block_rows].astype(jnp.float32)
    out[...] = total[...].astype(out.dtype)


def shards(queries, passages, candidates, positives, row_weight, owner_map):
    columns = lax.axis_size("dp")
    groups = lax.axis_size("group")
    devices = columns * groups
    query_blocks, block_rows, width = queries.shape
    rows = query_blocks * block_rows
    blocks = passages.shape[0]
    listed = candidates.shape[1]
    near_cap = (NLOCAL + columns - 1) // columns
    far_cap = (listed - NLOCAL + groups - 2) // (groups - 1)
    cap = max(near_cap, far_cap)
    scale = 3.0 / math.sqrt(width)
    dtype = passages.dtype
    slots = columns * near_cap + (groups - 1) * far_cap
    table_rows = -(-(1 + query_blocks) * cap // 8) * 8
    all_lists = devices * query_blocks

    far_queries = {0: queries}
    far_queries[groups - 1] = swap(queries, "group", groups - 1)
    mask = groups // 2 - 1
    if mask:
        far_queries[mask] = swap(queries, "group", mask)
    near_queries = [queries] + [swap(queries, "dp", mask) for mask in range(2, columns, 2)]

    vmem = pl.BlockSpec(memory_space=pltpu.VMEM)
    hbm = pl.BlockSpec(memory_space=pltpu.HBM)
    far_shape = jax.ShapeDtypeStruct((far_cap, block_rows, width), dtype)
    *far_out, near_out, asked, numbers, row_data = pl.pallas_call(
        functools.partial(
            plan_kernel, scale, cap, near_cap, far_cap, columns, groups, query_blocks
        ),
        out_shape=[far_shape] * (groups - 1)
        + [
            jax.ShapeDtypeStruct((columns * near_cap, block_rows, width), dtype),
            jax.ShapeDtypeStruct((table_rows, all_lists), jnp.int32),
            jax.ShapeDtypeStruct((8, slots * block_rows), jnp.float32),
            jax.ShapeDtypeStruct((8, rows), jnp.float32),
        ],
        in_specs=[hbm] * 5,
        out_specs=[hbm] * groups + [vmem] * 3,
        scratch_shapes=[
            pltpu.VMEM((listed, all_lists), jnp.int32),
            pltpu.VMEM((1, owner_map.shape[0]), jnp.int32),
            pltpu.VMEM(row_weight.shape, jnp.float32),
            pltpu.VMEM(positives.shape, jnp.int32),
            pltpu.VMEM(passages.shape, dtype),
            pltpu.VMEM((table_rows, devices), jnp.int32),
            pltpu.SMEM((table_rows, all_lists), jnp.int32),
            pltpu.SMEM((table_rows, devices), jnp.int32),
            pltpu.SemaphoreType.DMA((5,)),
            pltpu.SemaphoreType.DMA((slots,)),
            pltpu.SemaphoreType.DMA((2,)),
        ],
        compiler_params=pltpu.CompilerParams(vmem_limit_bytes=PLAN_VMEM_BYTES),
        cost_estimate=pl.CostEstimate(flops=0, bytes_accessed=PLAN_BYTES, transcendentals=0),
    )(candidates.T, owner_map.reshape(1, -1), row_weight, positives, passages)
    farthest = far_queries.pop(groups - 1)
    farthest, near_queries, far_queries, far_out, near_out = lax.optimization_barrier(
        (farthest, near_queries[::-1], far_queries, far_out, near_out)
    )
    near_queries = near_queries[::-1]
    far_queries[groups - 1] = farthest
    far_blocks = [swap(far_out[mask - 1], "group", mask) for mask in range(1, groups)]
    near_blocks = lax.all_to_all(near_out, "dp", split_axis=0, concat_axis=0, tiled=True)
    mask = groups // 2 - 1
    while mask:
        for at, piece in list(far_queries.items()):
            if at ^ mask not in far_queries:
                far_queries[at ^ mask] = swap(piece, "group", mask)
        mask >>= 1
    beside = swap(jnp.concatenate(near_queries), "dp", 1)

    near_slots, far_slots = columns * near_cap, (groups - 1) * far_cap
    near_stat, near_scores = local_call(
        functools.partial(near_kernel, scale, columns),
        [],
        [queries, numbers, near_blocks],
        [
            jax.ShapeDtypeStruct((rows, 128), jnp.float32),
            jax.ShapeDtypeStruct((rows, near_slots * block_rows), jnp.float32),
        ],
        [pltpu.VMEM((rows, block_rows), jnp.float32)],
        NEAR_BYTES,
    )
    stat, far_scores = local_call(
        functools.partial(stats_kernel, scale, near_slots * block_rows),
        [],
        [queries, row_data, numbers, near_stat, *far_blocks],
        [
            jax.ShapeDtypeStruct((8, rows), jnp.float32),
            jax.ShapeDtypeStruct((rows, far_slots * block_rows), jnp.float32),
        ],
        [pltpu.VMEM((rows, block_rows), jnp.float32)],
        0,
    )
    pair = jnp.stack([stat, swap(stat, "dp", 1)])
    near_stats = [pair] + [swap(pair, "dp", mask) for mask in range(2, columns, 2)]
    far_pair = jnp.stack([stat, swap(stat, "group", 1)])
    far_stats = [far_pair] + [swap(far_pair, "group", mask) for mask in range(2, groups, 2)]
    grad_query = local_call(
        functools.partial(query_kernel, columns),
        [],
        [numbers, stat, near_scores, far_scores, near_blocks, *far_blocks],
        jax.ShapeDtypeStruct(queries.shape, dtype),
        [
            pltpu.VMEM((rows, width), jnp.float32),
            pltpu.VMEM((rows, cap * block_rows), dtype),
        ],
        2 * VMEM_BYTES,
    )

    query_inputs = near_queries + [beside] + [far_queries[mask] for mask in range(1, groups)]
    stat_inputs = near_stats + far_stats

    def unit_of(unit, queries_in, stats_in):
        pairs = columns // 2
        if unit >= columns:
            far = unit - columns
            place = (far + 1) // 2
            return queries_in[pairs + 1 + far], stats_in[pairs + place].at[(far + 1) % 2]
        stat = stats_in[unit // 2].at[unit % 2]
        if unit % 2 == 0:
            return queries_in[unit // 2], stat
        return queries_in[pairs].at[pl.ds(unit // 2 * query_blocks, query_blocks)], stat

    grad_passage = local_call(
        functools.partial(
            passage_kernel,
            scale,
            cap,
            near_cap,
            far_cap,
            columns,
            groups,
            unit_of,
            (len(query_inputs), len(stat_inputs)),
        ),
        [asked],
        [passages, *query_inputs, *stat_inputs],
        jax.ShapeDtypeStruct(passages.shape, dtype),
        [pltpu.VMEM(passages.shape, jnp.float32)],
        0,
    )
    return (grad_query, grad_passage)


def solution(mesh):
    return jax.shard_map(
        shards,
        mesh=mesh,
        in_specs=(
            P(("group", "dp"), None, None),
            P(("group", "dp"), None, None),
            P(),
            P(("group", "dp"), None),
            P(("group", "dp"), None),
            P(),
        ),
        out_specs=(P(("group", "dp"), None, None), P(("group", "dp"), None, None)),
        check_vma=False,
    )
```

```python
import functools
import math

import jax
import jax.numpy as jnp
from jax import lax
from jax.experimental import pallas as pl
from jax.experimental.pallas import tpu as pltpu
from jax.sharding import PartitionSpec as P

NLOCAL = 12
VMEM_BYTES = 32 * 1024 * 1024
PLAN_VMEM_BYTES = 63 * 1024 * 1024
PLAN_BYTES = 16 * 1024 * 1024
NEAR_BYTES = 64 * 1024 * 1024


def swap(x, axis, mask):
    size = lax.axis_size(axis)
    return lax.ppermute(x, axis, [(i, i ^ mask) for i in range(size)])


def local_call(kernel, tables, inputs, outs, scratch, cost):
    smem = pl.BlockSpec(memory_space=pltpu.SMEM)
    vmem = pl.BlockSpec(memory_space=pltpu.VMEM)
    return pl.pallas_call(
        kernel,
        out_shape=outs,
        in_specs=[smem] * len(tables) + [vmem] * len(inputs),
        out_specs=jax.tree.map(lambda _: vmem, outs),
        scratch_shapes=scratch,
        compiler_params=pltpu.CompilerParams(vmem_limit_bytes=VMEM_BYTES),
        cost_estimate=pl.CostEstimate(flops=0, bytes_accessed=cost, transcendentals=0),
    )(*tables, *inputs)


def start_all(pairs, sems):
    copies = [
        pltpu.make_async_copy(source, target, sems.at[index])
        for index, (source, target) in enumerate(pairs)
    ]
    for copy in copies:
        copy.start()
    return copies


def owners_of(columns, groups):
    group, column = lax.axis_index("group"), lax.axis_index("dp")
    near = [group * columns + (column ^ mask) for mask in range(columns)]
    far = [(group ^ mask) * columns + column for mask in range(1, groups)]
    return near, far


def slot_rows(listings, cap, devices_of):
    query_blocks = len(listings[0])
    shape = listings[0][0].shape
    held = [jnp.zeros(shape, jnp.float32) for _ in range(cap)]
    entry = [jnp.full(shape, -1.0, jnp.float32) for _ in range(query_blocks * cap)]
    rank = jnp.zeros(shape, jnp.float32)
    for index, listing in enumerate(listings):
        listed = devices_of(functools.reduce(jnp.maximum, listing) >= 0.0)
        for slot in range(cap):
            here = listed & (rank == slot)
            held[slot] = jnp.where(here, float(index), held[slot])
            for block in range(query_blocks):
                at = block * cap + slot
                entry[at] = jnp.where(here, listing[block], entry[at])
        rank = rank + jnp.where(listed, 1.0, 0.0)
    return held + entry


def write_rows(rows, out):
    out[...] = jnp.zeros_like(out)
    for index, row in enumerate(rows):
        out[index : index + 1] = row.astype(jnp.int32)


def plan_kernel(scale, cap, near_cap, far_cap, columns, groups, query_blocks, *refs):
    lists_in, owners_in, weight_in, positives_in, passages_in = refs[:5]
    fars, (near_out, asked, numbers, row_data) = refs[5 : 4 + groups], refs[4 + groups : 8 + groups]
    lists, owners, weight, positives, passages, wanted = refs[8 + groups : 14 + groups]
    scalars, wanted_scalars, sems, out_sems, scalar_sems = refs[14 + groups :]
    loads = start_all(
        (
            (lists_in, lists),
            (owners_in, owners),
            (passages_in, passages),
            (weight_in, weight),
            (positives_in, positives),
        ),
        sems,
    )
    devices = columns * groups
    blocks = passages.shape[0]
    listed, lanes = lists.shape
    group, column = lax.axis_index("group"), lax.axis_index("dp")
    device = group * columns + column
    loads[0].wait()
    loads[1].wait()
    number = lax.broadcasted_iota(jnp.int32, (listed, lanes), 0).astype(jnp.float32)
    ids = lax.broadcasted_iota(jnp.int32, owners.shape, 1)
    listings = []
    for block in range(blocks):
        here = owners[...] == device * blocks + block
        block_id = jnp.max(jnp.where(here, ids, 0).astype(jnp.float32), axis=1, keepdims=True)
        match = lists[...] == block_id.astype(jnp.int32)
        listings.append([jnp.max(jnp.where(match, number, -1.0), axis=0, keepdims=True)])
    lane = lax.broadcasted_iota(jnp.int32, (1, lanes), 1)
    place_in = lax.rem(lane, query_blocks)

    def of_device(flags):
        value = jnp.where(flags, 1.0, 0.0)
        most = value
        for other in range(1, query_blocks):
            ahead = jnp.concatenate([value[:, other:], value[:, :other]], axis=1)
            behind = jnp.concatenate([value[:, -other:], value[:, :-other]], axis=1)
            most = jnp.maximum(most, jnp.where(place_in + other < query_blocks, ahead, 0.0))
            most = jnp.maximum(most, jnp.where(place_in >= other, behind, 0.0))
        return most > 0.0

    write_rows(slot_rows(listings, cap, of_device), asked)
    to_scalars = pltpu.make_async_copy(asked, scalars, scalar_sems.at[0])
    to_scalars.start()
    loads[2].wait()
    to_scalars.wait()
    pairs = []
    near, far = owners_of(columns, groups)
    for out, owner in zip(fars, far):
        for slot in range(far_cap):
            pairs.append((passages.at[scalars[slot, owner * query_blocks]], out.at[slot]))
    for peer in range(columns):
        owner = group * columns + peer
        for slot in range(near_cap):
            source = passages.at[scalars[slot, owner * query_blocks]]
            pairs.append((source, near_out.at[peer * near_cap + slot]))
    copies = start_all(pairs, out_sems)
    lane = lax.broadcasted_iota(jnp.int32, (listed, lanes), 1)
    place = lax.broadcasted_iota(jnp.int32, (listed, owners.shape[1]), 1)
    first = lax.broadcasted_iota(jnp.int32, (listed, devices), 1) * blocks
    number = lax.broadcasted_iota(jnp.int32, (listed, devices), 0).astype(jnp.float32)
    positions = []
    for block in range(query_blocks):
        mine = jnp.where(lane == device * query_blocks + block, lists[...], 0)
        mine = jnp.max(mine.astype(jnp.float32), axis=1, keepdims=True).astype(jnp.int32)
        found = jnp.where(place == mine, owners[...], 0).astype(jnp.float32)
        positions.append(jnp.max(found, axis=1, keepdims=True).astype(jnp.int32))
    listings = [
        [
            jnp.max(jnp.where(position == first + block, number, -1.0), axis=0, keepdims=True)
            for position in positions
        ]
        for block in range(blocks)
    ]
    write_rows(slot_rows(listings, cap, lambda flags: flags)[cap:], wanted)
    to_scalars = pltpu.make_async_copy(wanted, wanted_scalars, scalar_sems.at[1])
    to_scalars.start()
    loads[3].wait()
    loads[4].wait()
    row_data[...] = jnp.zeros_like(row_data)
    block_rows = weight.shape[1]
    for block in range(query_blocks):
        mine = slice(block * block_rows, (block + 1) * block_rows)
        row_data[2:3, mine] = weight[block : block + 1] * scale
        row_data[3:4, mine] = positives[block : block + 1].astype(jnp.float32)
    to_scalars.wait()
    numbers[...] = jnp.full_like(numbers, -1.0)
    place = lax.broadcasted_iota(jnp.int32, (1, block_rows), 1)
    entries = [(group * columns + peer, slot) for peer in range(columns) for slot in range(near_cap)]
    entries += [(owner, slot) for owner in far for slot in range(far_cap)]
    for index, (owner, slot) in enumerate(entries):
        for block in range(query_blocks):
            listing = wanted_scalars[block * cap + slot, owner]
            number = jnp.where(listing >= 0, place + listing * block_rows, -1)
            numbers[block : block + 1, index * block_rows : (index + 1) * block_rows] = (
                number.astype(jnp.float32)
            )
    for copy in copies:
        copy.wait()


def score_blocks(scale, queries, pieces, numbers, first, scores, peak_ref):
    query_blocks, block_rows, width = queries.shape
    rows = query_blocks * block_rows
    query = queries[...].reshape(rows, width)
    peak_ref[...] = jnp.full_like(peak_ref, -jnp.inf)
    at = 0
    for piece in pieces:
        size = piece.shape[0]
        part = lax.dot_general(
            query, piece, (((1,), (1,)), ((), ())), preferred_element_type=jnp.float32
        )
        for block in range(query_blocks):
            mine = slice(block * block_rows, (block + 1) * block_rows)
            number = numbers[block : block + 1, first + at : first + at + size]
            own = jnp.where(number >= 0.0, part[mine] * scale, -jnp.inf)
            scores[mine, at : at + size] = own
            peak = peak_ref[mine]
            for column in range(0, size, block_rows):
                peak = jnp.maximum(peak, own[:, column : column + block_rows])
            peak_ref[mine] = peak
        at += size
    peak = jnp.max(peak_ref[...], axis=1, keepdims=True)
    total = jnp.zeros((rows, block_rows), jnp.float32)
    for column in range(0, at, block_rows):
        total = total + jnp.exp(scores[:, column : column + block_rows] - peak)
    return peak, jnp.sum(total, axis=1, keepdims=True)


def near_pieces(near, columns):
    cap = near.shape[0] // columns
    for peer in range(columns):
        yield near[peer * cap : (peer + 1) * cap].reshape(-1, near.shape[-1])


def far_pieces(fars):
    for ref in fars[::-1]:
        yield ref[...].reshape(-1, ref.shape[-1])


def near_kernel(scale, columns, queries, numbers, near, out, scores, peak_ref):
    pieces = near_pieces(near, columns)
    peak, total = score_blocks(scale, queries, pieces, numbers, 0, scores, peak_ref)
    lane = lax.broadcasted_iota(jnp.int32, out.shape, 1)
    out[...] = jnp.where(lane == 0, peak, total)


def stats_kernel(scale, first, queries, row_data, numbers, near_stat, *refs):
    fars, (stat, scores, peak_ref) = refs[:-3], refs[-3:]
    far_peak, far_total = score_blocks(
        scale, queries, far_pieces(fars), numbers, first, scores, peak_ref
    )
    near_peak, near_total = near_stat[:, 0:1], near_stat[:, 1:2]
    peak = jnp.maximum(near_peak, far_peak)
    total = near_total * jnp.exp(near_peak - peak) + far_total * jnp.exp(far_peak - peak)
    lane = lax.broadcasted_iota(jnp.int32, (peak.shape[0], 128), 1)
    turned = jnp.where(lane == 0, peak, total).T
    stat[...] = row_data[...]
    stat[0:2] = turned[0:2]


def query_kernel(columns, numbers, stat, near_scores, far_scores, near, *refs):
    fars, (out, total, dscore_ref) = refs[:-3], refs[-3:]
    query_blocks, block_rows, width = out.shape
    rows = query_blocks * block_rows
    turned = jnp.concatenate(
        [stat[...], jnp.zeros((128 - stat.shape[0], rows), jnp.float32)], axis=0
    ).T
    peak, inverse = turned[:, 0:1], 1.0 / turned[:, 1:2]
    weight, positive = turned[:, 2:3], turned[:, 3:4]
    total[...] = jnp.zeros_like(total)
    first = 0
    for scores, pieces in ((near_scores, near_pieces(near, columns)), (far_scores, far_pieces(fars))):
        at = 0
        for piece in pieces:
            size = piece.shape[0]
            for block in range(query_blocks):
                mine = slice(block * block_rows, (block + 1) * block_rows)
                number = numbers[block : block + 1, first + at : first + at + size]
                chance = jnp.exp(scores[mine, at : at + size] - peak[mine]) * inverse[mine]
                target = jnp.where(positive[mine] == number, 1.0, 0.0)
                dscore_ref[mine, :size] = ((chance - target) * weight[mine]).astype(jnp.bfloat16)
            total[...] += jnp.dot(
                dscore_ref[:, :size], piece, preferred_element_type=jnp.float32
            )
            at += size
        first += at
    out[...] = total[...].reshape(out.shape).astype(out.dtype)


def passage_kernel(scale, cap, near_cap, far_cap, columns, groups, unit_of, counts, *refs):
    asked, passages = refs[:2]
    query_count, stat_count = counts
    queries_in = refs[2 : 2 + query_count]
    stats_in = refs[2 + query_count : 2 + query_count + stat_count]
    out, total = refs[2 + query_count + stat_count :]
    near, far = owners_of(columns, groups)
    units = [(owner, near_cap) for owner in near] + [(owner, far_cap) for owner in far]
    query_blocks, block_rows, width = queries_in[0].shape
    rows = query_blocks * block_rows
    total[...] = jnp.zeros_like(total)
    lane = lax.broadcasted_iota(jnp.int32, (1, rows), 1)
    place = lax.broadcasted_iota(jnp.int32, (block_rows, rows), 0).astype(jnp.float32)
    for unit, (owner, slots) in enumerate(units):
        query, stat = unit_of(unit, queries_in, stats_in)
        query = query[...].reshape(rows, width)
        peak, weight, positive = stat[0:1], stat[2:3], stat[3:4]
        share = weight / stat[1:2]
        held = [asked[slot, owner * query_blocks] for slot in range(slots)]
        mine = jnp.concatenate([passages[index] for index in held], axis=0)
        scores = (
            lax.dot_general(
                mine, query, (((1,), (1,)), ((), ())), preferred_element_type=jnp.float32
            )
            * scale
        )
        parts = []
        for slot in range(slots):
            listing = jnp.full((1, rows), asked[cap + slot, owner * query_blocks], jnp.int32)
            for block in range(1, query_blocks):
                later = asked[cap + slot, owner * query_blocks + block]
                listing = jnp.where(lane >= block * block_rows, later, listing)
            bias = jnp.where(listing >= 0, -peak, -jnp.inf)
            row = positive - (listing * block_rows).astype(jnp.float32)
            part = scores[slot * block_rows : (slot + 1) * block_rows]
            target = jnp.where(row == place, weight, 0.0)
            parts.append((jnp.exp(part + bias) * share - target).astype(jnp.bfloat16))
        term = jnp.dot(
            jnp.concatenate(parts, axis=0), query, preferred_element_type=jnp.float32
        ).astype(jnp.bfloat16)
        for slot, index in enumerate(held):
            total[index] += term[slot * block_rows : (slot + 1) * block_rows].astype(jnp.float32)
    out[...] = total[...].astype(out.dtype)


def shards(queries, passages, candidates, positives, row_weight, owner_map):
    columns = lax.axis_size("dp")
    groups = lax.axis_size("group")
    devices = columns * groups
    query_blocks, block_rows, width = queries.shape
    rows = query_blocks * block_rows
    blocks = passages.shape[0]
    listed = candidates.shape[1]
    near_cap = (NLOCAL + columns - 1) // columns
    far_cap = (listed - NLOCAL + groups - 2) // (groups - 1)
    cap = max(near_cap, far_cap)
    scale = 3.0 / math.sqrt(width)
    dtype = passages.dtype
    slots = columns * near_cap + (groups - 1) * far_cap
    table_rows = -(-(1 + query_blocks) * cap // 8) * 8
    all_lists = devices * query_blocks

    far_queries = {0: queries}
    far_queries[groups - 1] = swap(queries, "group", groups - 1)
    mask = groups // 2 - 1
    if mask:
        far_queries[mask] = swap(queries, "group", mask)
    near_queries = [queries] + [swap(queries, "dp", mask) for mask in range(2, columns, 2)]

    vmem = pl.BlockSpec(memory_space=pltpu.VMEM)
    hbm = pl.BlockSpec(memory_space=pltpu.HBM)
    far_shape = jax.ShapeDtypeStruct((far_cap, block_rows, width), dtype)
    *far_out, near_out, asked, numbers, row_data = pl.pallas_call(
        functools.partial(
            plan_kernel, scale, cap, near_cap, far_cap, columns, groups, query_blocks
        ),
        out_shape=[far_shape] * (groups - 1)
        + [
            jax.ShapeDtypeStruct((columns * near_cap, block_rows, width), dtype),
            jax.ShapeDtypeStruct((table_rows, all_lists), jnp.int32),
            jax.ShapeDtypeStruct((8, slots * block_rows), jnp.float32),
            jax.ShapeDtypeStruct((8, rows), jnp.float32),
        ],
        in_specs=[hbm] * 5,
        out_specs=[hbm] * groups + [vmem] * 3,
        scratch_shapes=[
            pltpu.VMEM((listed, all_lists), jnp.int32),
            pltpu.VMEM((1, owner_map.shape[0]), jnp.int32),
            pltpu.VMEM(row_weight.shape, jnp.float32),
            pltpu.VMEM(positives.shape, jnp.int32),
            pltpu.VMEM(passages.shape, dtype),
            pltpu.VMEM((table_rows, devices), jnp.int32),
            pltpu.SMEM((table_rows, all_lists), jnp.int32),
            pltpu.SMEM((table_rows, devices), jnp.int32),
            pltpu.SemaphoreType.DMA((5,)),
            pltpu.SemaphoreType.DMA((slots,)),
            pltpu.SemaphoreType.DMA((2,)),
        ],
        compiler_params=pltpu.CompilerParams(vmem_limit_bytes=PLAN_VMEM_BYTES),
        cost_estimate=pl.CostEstimate(flops=0, bytes_accessed=PLAN_BYTES, transcendentals=0),
    )(candidates.T, owner_map.reshape(1, -1), row_weight, positives, passages)
    farthest = far_queries.pop(groups - 1)
    farthest, near_queries, far_queries, far_out, near_out = lax.optimization_barrier(
        (farthest, near_queries[::-1], far_queries, far_out, near_out)
    )
    near_queries = near_queries[::-1]
    far_queries[groups - 1] = farthest
    far_blocks = [swap(far_out[mask - 1], "group", mask) for mask in range(1, groups)]
    near_blocks = lax.all_to_all(near_out, "dp", split_axis=0, concat_axis=0, tiled=True)
    mask = groups // 2 - 1
    while mask:
        for at, piece in list(far_queries.items()):
            if at ^ mask not in far_queries:
                far_queries[at ^ mask] = swap(piece, "group", mask)
        mask >>= 1
    beside = swap(jnp.concatenate(near_queries), "dp", 1)

    near_slots, far_slots = columns * near_cap, (groups - 1) * far_cap
    near_stat, near_scores = local_call(
        functools.partial(near_kernel, scale, columns),
        [],
        [queries, numbers, near_blocks],
        [
            jax.ShapeDtypeStruct((rows, 128), jnp.float32),
            jax.ShapeDtypeStruct((rows, near_slots * block_rows), jnp.float32),
        ],
        [pltpu.VMEM((rows, block_rows), jnp.float32)],
        NEAR_BYTES,
    )
    stat, far_scores = local_call(
        functools.partial(stats_kernel, scale, near_slots * block_rows),
        [],
        [queries, row_data, numbers, near_stat, *far_blocks[::-1]],
        [
            jax.ShapeDtypeStruct((8, rows), jnp.float32),
            jax.ShapeDtypeStruct((rows, far_slots * block_rows), jnp.float32),
        ],
        [pltpu.VMEM((rows, block_rows), jnp.float32)],
        0,
    )
    pair = jnp.stack([stat, swap(stat, "dp", 1)])
    near_stats = [pair] + [swap(pair, "dp", mask) for mask in range(2, columns, 2)]
    far_pair = jnp.stack([stat, swap(stat, "group", 1)])
    far_stats = [far_pair] + [swap(far_pair, "group", mask) for mask in range(2, groups, 2)]
    grad_query = local_call(
        functools.partial(query_kernel, columns),
        [],
        [numbers, stat, near_scores, far_scores, near_blocks, *far_blocks[::-1]],
        jax.ShapeDtypeStruct(queries.shape, dtype),
        [
            pltpu.VMEM((rows, width), jnp.float32),
            pltpu.VMEM((rows, cap * block_rows), dtype),
        ],
        2 * VMEM_BYTES,
    )

    query_inputs = near_queries + [beside] + [far_queries[mask] for mask in range(1, groups)]
    stat_inputs = near_stats + far_stats

    def unit_of(unit, queries_in, stats_in):
        pairs = columns // 2
        if unit >= columns:
            far = unit - columns
            place = (far + 1) // 2
            return queries_in[pairs + 1 + far], stats_in[pairs + place].at[(far + 1) % 2]
        stat = stats_in[unit // 2].at[unit % 2]
        if unit % 2 == 0:
            return queries_in[unit // 2], stat
        return queries_in[pairs].at[pl.ds(unit // 2 * query_blocks, query_blocks)], stat

    grad_passage = local_call(
        functools.partial(
            passage_kernel,
            scale,
            cap,
            near_cap,
            far_cap,
            columns,
            groups,
            unit_of,
            (len(query_inputs), len(stat_inputs)),
        ),
        [asked],
        [passages, *query_inputs, *stat_inputs],
        jax.ShapeDtypeStruct(passages.shape, dtype),
        [pltpu.VMEM(passages.shape, jnp.float32)],
        0,
    )
    return (grad_query, grad_passage)


def solution(mesh):
    return jax.shard_map(
        shards,
        mesh=mesh,
        in_specs=(
            P(("group", "dp"), None, None),
            P(("group", "dp"), None, None),
            P(),
            P(("group", "dp"), None),
            P(("group", "dp"), None),
            P(),
        ),
        out_specs=(P(("group", "dp"), None, None), P(("group", "dp"), None, None)),
        check_vma=False,
    )
```
